512 devices in a mesh: blk: 16 (over x, y_lo, core), bulk: 32 (over z, y_hi).
Axes of the slice: x: 4, y: 4 (y_hi: 2, y_lo: 2; y = y_hi * 2 + y_lo), z: 16, core: 2. Of those that a mesh axis runs over, the one named last changes fastest.
Arguments:
- targets: float32 [16, 128, 96, 192], P('blk', 'bulk'), may hold values from -1.5 to 1.5
- sources: float32 [16, 128, 96, 192], P('blk', 'bulk'), may hold values from -1.5 to 1.5
- permittivity: float32 [128, 96, 192], P('bulk'), may hold values from 2 to 4
Outputs:
- exchange_action: float32 [16, 128, 96, 192], P('blk', 'bulk')
The draws below stay inside these ranges and needn't reach their ends.
All inputs are finite; a program needn't handle non-finite values.
Results may differ from the reference program's by a relative error of at most 0.0003.
Values sent between devices are 32-bit elements; how exact they have to be, the bound alone decides.
A program may use at most 64 MiB of HBM per device.

```python
import math
import jax
import jax.numpy as jnp
from jax import lax

ORB_BLOCK = 1
LINES_X = 96
LINES_Y = 192
SWEEPS = 3
CYCLE_STEPS = 2
ORBITALS = 16
GRID_Z = 128
N_BLK = 16


def signed_values(key, positive):
    sign_key, magnitude_key = jax.random.split(key)
    grid_shape = (ORBITALS, GRID_Z, LINES_X, LINES_Y)
    sign_part = jnp.where(jax.random.uniform(sign_key, grid_shape, jnp.float32) < positive, 1.0, -1.0)
    magnitude = jax.random.uniform(magnitude_key, grid_shape, jnp.float32, 1.0, 1.5)
    return (sign_part * magnitude).astype(jnp.float32)


def draw_targets(key, part):
    key = jax.random.fold_in(key, 11)
    return signed_values(key, 0.5)


def draw_sources(key, part):
    key = jax.random.fold_in(key, 23)
    return signed_values(key, 0.5)


def steps_of(own_key, extent, shards, low, high):
    def one(axis_at, shards_of):
        draws = jax.random.uniform(jax.random.fold_in(jax.random.fold_in(own_key, 6), axis_at), (shards_of,), jnp.float32, low / len(shards), high / len(shards))
        return jnp.repeat(jnp.exp(draws), extent[axis_at] // shards_of).reshape((-1,) + (1,) * (len(extent) - axis_at - 1))

    loudness = one(*shards[0])
    for cut in shards[1:]:
        loudness = loudness * one(*cut)
    return loudness


def setup_inputs(seed: int = 0) -> dict:
    key_list = jax.random.split(jax.random.key(seed), 4)
    return {
        "targets": draw_targets(jax.random.fold_in(key_list[3], 71), 0),
        "sources": draw_sources(jax.random.fold_in(key_list[3], 71), 0),
        "permittivity": jnp.clip(jnp.exp(math.log(4.0) - 0.6931472 * jax.random.uniform(key_list[2], (GRID_Z, LINES_X, LINES_Y), jnp.float32) ** steps_of(key_list[2], (GRID_Z, LINES_X, LINES_Y), ((0, 32),), -0.2, 0.2)), 2.0, 4.0),
    }


source_scale = math.pi


def coefficients(perm):
    ahead_x = 0.5 * (perm + jnp.roll(perm, -1, 1))
    ahead_y = 0.5 * (perm + jnp.roll(perm, -1, 2))
    ahead_z = 0.5 * (perm + jnp.roll(perm, -1, 0))
    behind_x = jnp.roll(ahead_x, 1, 1)
    behind_y = jnp.roll(ahead_y, 1, 2)
    behind_z = jnp.roll(ahead_z, 1, 0)
    diagonal = ahead_x + behind_x + ahead_y + behind_y + ahead_z + behind_z
    return (ahead_x, behind_x, ahead_y, behind_y, ahead_z, behind_z, diagonal)


def smooth(field, rhs, coefs):
    ahead_x, behind_x, ahead_y, behind_y, ahead_z, behind_z, diagonal = coefs
    near = ahead_x * jnp.roll(field, -1, -2) + behind_x * jnp.roll(field, 1, -2)
    near = near + ahead_y * jnp.roll(field, -1, -1) + behind_y * jnp.roll(field, 1, -1)
    near = near + ahead_z * jnp.roll(field, -1, -3) + behind_z * jnp.roll(field, 1, -3)
    return (rhs + near) / diagonal


def reference(targets, sources, permittivity):
    coefs = coefficients(permittivity)
    target_blocks = targets.reshape(N_BLK, ORB_BLOCK, GRID_Z, LINES_X, LINES_Y)
    source_blocks = sources.reshape(N_BLK, ORB_BLOCK, GRID_Z, LINES_X, LINES_Y)

    def one_block(block_index):
        own = lax.dynamic_index_in_dim(target_blocks, block_index, 0, keepdims=False)
        total = jnp.zeros((ORB_BLOCK, GRID_Z, LINES_X, LINES_Y), jnp.float32)
        for cycle_step in range(1, CYCLE_STEPS + 1):
            where = ((block_index - cycle_step) % N_BLK).astype(jnp.int32)
            visit = lax.dynamic_index_in_dim(source_blocks, where, 0, keepdims=False)
            density = visit[:, None] * own[None]
            rhs = source_scale * density
            potential = rhs / coefs[6]
            for sweep_index in range(SWEEPS):
                potential = smooth(potential, rhs, coefs)
            total = total + jnp.sum(visit[:, None] * potential, axis=0)
        return -total

    result = lax.map(one_block, jnp.arange(N_BLK, dtype=jnp.int32))
    return result.reshape(ORBITALS, GRID_Z, LINES_X, LINES_Y)
```

```python
import functools
import math

import jax
import jax.numpy as jnp
from jax import lax
from jax.experimental import pallas as pl
from jax.experimental.pallas import tpu as pltpu
from jax.sharding import PartitionSpec as P

MESH = pl.DeviceIdType.MESH
SLAB = 4
WIDE = 256
SCALE = math.pi


def packed(plane):
    lines = plane.shape[0]
    right = plane[:, 128:192]
    return plane[:, 0:128], jnp.concatenate([right[: lines // 2], right[lines // 2 :]], axis=1)


def unpacked(both):
    lines = both.shape[0] * 2 // 3
    left, right = both[:lines], both[lines:]
    left_turned = pltpu.roll(left, 64, 1)
    right_turned = pltpu.roll(right, 64, 1)
    lane = lax.broadcasted_iota(jnp.int32, right.shape, 1)
    low = jnp.where(lane < 64, right, jnp.where(lane < 96, left_turned[: lines // 2], right_turned))
    high = jnp.where(lane < 64, right_turned, jnp.where(lane < 96, left_turned[lines // 2 :], right))
    return left, jnp.concatenate([low, high], axis=0)


def ahead(cells, axis):
    return pltpu.roll(cells, cells.shape[axis] - 1, axis)


def behind(cells, axis):
    return pltpu.roll(cells, 1, axis)


def kernel(
    n_blk, n_bulk,
    t_hbm, s_hbm, e_hbm, out_ref,
    t_in, s_in, e_in, own_s, tgt, direct, passed, eps, eps_wide, coef, inverse, first, mid, late,
    in_sem, send_sem, recv_sem,
):
    b, k = lax.axis_index("blk"), lax.axis_index("bulk")
    core, lo, hi = lax.rem(b, 2), lax.rem(b // 2, 2), lax.rem(k, 2)
    lines = t_in.shape[1]
    other_k = k + 1 - 2 * hi
    next_b, prev_b = lax.rem(b + 2, n_blk), lax.rem(b + n_blk - 2, n_blk)
    partner = (b, other_k)
    chip_mate = (b + 1 - 2 * core, k)
    next_same, next_other = (next_b, k), (next_b, other_k)
    prev_same, prev_other = (prev_b, k), (prev_b, other_k)
    beside = (b + 2 - 4 * lo, other_k)
    z_to = (b, lax.rem(k + n_bulk + 2 - 4 * hi, n_bulk))
    z_from = (b, lax.rem(k + n_bulk - 2 + 4 * hi, n_bulk))

    loads = [
        pltpu.make_async_copy(src, dst, in_sem.at[i])
        for i, (src, dst) in enumerate(((s_hbm.at[0], s_in), (t_hbm.at[0], t_in), (e_hbm, e_in)))
    ]
    for load in loads:
        load.start()

    barrier = pltpu.get_barrier_semaphore()

    def tell(devices):
        for device in devices:
            pl.semaphore_signal(barrier, inc=1, device_id=device, device_id_type=MESH)

    tell((partner, prev_same, prev_other, z_from, chip_mate))

    @pl.when(core == 0)
    def _():
        tell((beside,))

    own = 3 + hi
    far = 7 * (1 - hi)
    far_there = 7 * hi
    z_src, z_dst = 8 * (1 - hi), 8 * hi

    def pack(src, dst, at):
        def body(i, _):
            left, right = packed(src[i])
            dst[at + i, 0:lines] = left
            dst[at + i, lines:] = right
            return 0
        lax.fori_loop(0, SLAB, body, 0)

    loads[0].wait()
    pack(s_in, own_s, 0)
    loads[1].wait()
    pack(t_in, tgt, own)
    loads[2].wait()
    pack(e_in, eps, 4)

    @pl.when(core == 0)
    def _():
        pl.semaphore_wait(barrier, 6)

    @pl.when(core == 1)
    def _():
        pl.semaphore_wait(barrier, 5)

    def copy(i, src, src_at, dst, dst_at, count, device):
        return pltpu.make_async_remote_copy(
            src_ref=src.at[pl.ds(src_at, count)], dst_ref=dst.at[pl.ds(dst_at, count)],
            send_sem=send_sem.at[i], recv_sem=recv_sem.at[i], device_id=device, device_id_type=MESH,
        )

    tgt_far = copy(0, tgt, own, tgt, far_there, 4, partner)
    tgt_z = copy(1, tgt, z_src, tgt, z_dst, 3, z_to)
    direct_own = copy(2, own_s, 0, direct, own, 4, next_same)
    direct_far = copy(3, own_s, 0, direct, far_there, 4, next_other)
    direct_z = copy(4, direct, z_src, direct, z_dst, 3, z_to)
    eps_far = copy(5, eps, 4, eps, 8 * hi, 4, beside)
    eps_z = copy(6, eps, z_src, eps, z_dst, 4, z_to)
    mate_own_s = copy(7, own_s, 0, passed, own, 4, chip_mate)
    mate_eps_far = copy(8, eps, z_src, eps, z_src, 4, chip_mate)
    mate_eps_z = copy(9, eps, z_dst, eps, z_dst, 4, chip_mate)
    passed_far = copy(10, passed, own, passed, far_there, 4, partner)
    passed_z = copy(11, passed, z_src, passed, z_dst, 3, z_to)
    mate_direct_own = copy(7, direct, own, passed, own, 4, chip_mate)
    mate_direct_far = copy(8, direct, far, passed, far, 4, chip_mate)
    mate_direct_z = copy(9, direct, z_dst, passed, z_dst, 3, chip_mate)

    @pl.when(core == 0)
    def _():
        mate_own_s.start()
        eps_far.start()
        tgt_far.start()
        direct_far.start()
        direct_own.start()
        eps_far.wait_recv()
        eps_z.start()
        mate_eps_far.start()
        tgt_far.wait_recv()
        tgt_z.start()
        direct_far.wait_recv()
        direct_z.start()
        eps_z.wait_recv()
        mate_eps_z.start()

    @pl.when(core == 1)
    def _():
        tgt_far.start()
        direct_far.start()
        mate_own_s.wait_recv()
        passed_far.start()
        direct_own.start()
        tgt_far.wait_recv()
        tgt_z.start()
        direct_far.wait_recv()
        direct_z.start()
        mate_direct_far.start()
        passed_far.wait_recv()
        passed_z.start()
        direct_own.wait_recv()
        mate_direct_own.start()
        direct_z.wait_recv()
        mate_direct_z.start()
        mate_eps_far.wait_recv()
        mate_eps_z.wait_recv()

    def wide_body(i, _):
        left, right = unpacked(eps[i])
        eps_wide[i, :, 0:128] = left
        eps_wide[i, :, 128:WIDE] = right
        return 0

    lax.fori_loop(0, 12, wide_body, 0)

    def coef_body(i, _):
        cells = eps_wide[i + 1]
        ahead_x = 0.5 * (cells + ahead(cells, 0))
        ahead_y = 0.5 * (cells + ahead(cells, 1))
        ahead_z = 0.5 * (cells + eps_wide[i + 2])
        behind_x = behind(ahead_x, 0)
        behind_y = behind(ahead_y, 1)
        behind_z = 0.5 * (cells + eps_wide[i])
        inv = 1.0 / (ahead_x + behind_x + ahead_y + behind_y + ahead_z + behind_z)
        inverse[i] = SCALE * inv
        for j, face in enumerate((ahead_x, behind_x, ahead_y, behind_y, ahead_z, behind_z)):
            coef[j, i] = face * inv
        return 0

    lax.fori_loop(0, 10, coef_body, 0)

    def swept(src, i, start):
        cells = src[i]
        near = first[start] + coef[0, start] * ahead(cells, 0) + coef[1, start] * behind(cells, 0)
        near = near + coef[2, start] * ahead(cells, 1) + coef[3, start] * behind(cells, 1)
        return near + coef[4, start] * src[i + 1] + coef[5, start] * src[i - 1]

    def pair(source, add):
        def first_body(i, _):
            left, right = unpacked(source[i + hi] * tgt[i + hi])
            first[i, :, 0:128] = left * inverse[i, :, 0:128]
            first[i, :, 128:WIDE] = right * inverse[i, :, 128:WIDE]
            return 0

        lax.fori_loop(0, 10, first_body, 0)

        def mid_body(i, _):
            mid[i] = swept(first, i + 1, i + 1)
            return 0

        lax.fori_loop(0, 8, mid_body, 0)

        def late_body(i, _):
            late[i] = swept(mid, i + 1, i + 2)
            return 0

        lax.fori_loop(0, 6, late_body, 0)

        def out_body(i, _):
            potential = swept(late, i + 1, i + 3)
            left, right = unpacked(source[own + i])
            left = left * potential[:, 0:128]
            right = right[:, 0:64] * potential[:, 128:192]
            if add:
                out_ref[0, i, :, 0:128] = out_ref[0, i, :, 0:128] - left
                out_ref[0, i, :, 128:192] = out_ref[0, i, :, 128:192] - right
            else:
                out_ref[0, i, :, 0:128] = -left
                out_ref[0, i, :, 128:192] = -right
            return 0

        lax.fori_loop(0, SLAB, out_body, 0)

    tgt_z.wait_recv()

    @pl.when(core == 0)
    def _():
        direct_own.wait_recv()
        direct_z.wait_recv()

    pair(direct, False)

    @pl.when(core == 0)
    def _():
        mate_direct_own.wait_recv()
        mate_direct_far.wait_recv()
        mate_direct_z.wait_recv()

    @pl.when(core == 1)
    def _():
        passed_z.wait_recv()

    pair(passed, True)

    for sent in (tgt_far, tgt_z, direct_own, direct_far, direct_z):
        sent.wait_send()

    @pl.when(core == 0)
    def _():
        for sent in (eps_far, eps_z, mate_own_s, mate_eps_far, mate_eps_z):
            sent.wait_send()

    @pl.when(core == 1)
    def _():
        for sent in (passed_far, passed_z, mate_direct_own, mate_direct_far, mate_direct_z):
            sent.wait_send()


def shards(n_blk, n_bulk, targets, sources, permittivity):
    _, planes, lines, cells = targets.shape
    rows = lines * cells // 128

    def plane_stack(count, *tile):
        return pltpu.VMEM((count, *tile), jnp.float32)

    return pl.pallas_call(
        functools.partial(kernel, n_blk, n_bulk),
        out_shape=jax.ShapeDtypeStruct(targets.shape, jnp.float32),
        in_specs=[pl.BlockSpec(memory_space=pl.ANY)] * 3,
        out_specs=pl.BlockSpec(memory_space=pltpu.VMEM),
        scratch_shapes=[
            plane_stack(planes, lines, cells),
            plane_stack(planes, lines, cells),
            plane_stack(planes, lines, cells),
            plane_stack(planes, rows, 128),
            plane_stack(11, rows, 128),
            plane_stack(11, rows, 128),
            plane_stack(11, rows, 128),
            plane_stack(12, rows, 128),
            plane_stack(12, lines, WIDE),
            pltpu.VMEM((6, 10, lines, WIDE), jnp.float32),
            plane_stack(10, lines, WIDE),
            plane_stack(10, lines, WIDE),
            plane_stack(8, lines, WIDE),
            plane_stack(6, lines, WIDE),
            pltpu.SemaphoreType.DMA((3,)),
            pltpu.SemaphoreType.DMA((12,)),
            pltpu.SemaphoreType.DMA((12,)),
        ],
        compiler_params=pltpu.CompilerParams(collective_id=0, has_side_effects=True, vmem_limit_bytes=40 << 20),
        cost_estimate=pl.CostEstimate(flops=20_000_000, bytes_accessed=1_200_000, transcendentals=0),
    )(targets, sources, permittivity)


def solution(mesh):
    in_specs = (P("blk", "bulk", None, None), P("blk", "bulk", None, None), P("bulk", None, None))
    out_specs = P("blk", "bulk", None, None)
    return jax.shard_map(
        functools.partial(shards, mesh.shape["blk"], mesh.shape["bulk"]),
        mesh=mesh, in_specs=in_specs, out_specs=out_specs, check_vma=False,
    )
```

```python
import functools
import math

import jax
import jax.numpy as jnp
from jax import lax
from jax.experimental import pallas as pl
from jax.experimental.pallas import tpu as pltpu
from jax.sharding import PartitionSpec as P

MESH = pl.DeviceIdType.MESH
SLAB = 4
WIDE = 256
SCALE = math.pi


def packed(plane):
    lines = plane.shape[0]
    right = plane[:, 128:192]
    return plane[:, 0:128], jnp.concatenate([right[: lines // 2], right[lines // 2 :]], axis=1)


def unpacked(both):
    lines = both.shape[0] * 2 // 3
    left, right = both[:lines], both[lines:]
    left_turned = pltpu.roll(left, 64, 1)
    right_turned = pltpu.roll(right, 64, 1)
    lane = lax.broadcasted_iota(jnp.int32, right.shape, 1)
    low = jnp.where(lane < 64, right, jnp.where(lane < 96, left_turned[: lines // 2], right_turned))
    high = jnp.where(lane < 64, right_turned, jnp.where(lane < 96, left_turned[lines // 2 :], right))
    return left, jnp.concatenate([low, high], axis=0)


def ahead(cells, axis):
    return pltpu.roll(cells, cells.shape[axis] - 1, axis)


def behind(cells, axis):
    return pltpu.roll(cells, 1, axis)


def kernel(
    n_blk, n_bulk,
    t_hbm, s_hbm, e_hbm, out_ref,
    t_in, s_in, e_in, own_s, own_t, tgt, near_s, next_s, eps, done, back, eps_wide, coef, inverse, first, mid, late, total,
    in_sem, send_sem, recv_sem,
):
    b, k = lax.axis_index("blk"), lax.axis_index("bulk")
    pos, core, z, hi = b // 2, lax.rem(b, 2), k // 2, lax.rem(k, 2)
    n_pos = n_blk // 2
    lines = t_in.shape[1]
    home = core == hi
    away = core != hi
    prev_pos, next_pos = lax.rem(pos + n_pos - 1, n_pos), lax.rem(pos + 1, n_pos)
    mate = (b + 1 - 2 * core, k)
    beyond = (b + 1 - 2 * core, lax.rem(k + n_bulk - 2 + 4 * core, n_bulk))
    swap = (b + 1 - 2 * core, k + 1 - 2 * hi)
    beside = (b + 2 - 4 * lax.rem(pos, 2), k + 1 - 2 * hi)
    to_one = (lax.rem(pos + core, n_pos) * 2 + hi, 2 * z + 1 - core)
    to_two = (next_pos * 2 + hi, 2 * z + core)
    from_one = (lax.rem(pos + n_pos - 1 + hi, n_pos) * 2 + 1 - hi, 2 * z + core)
    from_two = (prev_pos * 2 + hi, 2 * z + core)

    loads = [
        pltpu.make_async_copy(src, dst, in_sem.at[i])
        for i, (src, dst) in enumerate(((s_hbm.at[0], s_in), (t_hbm.at[0], t_in), (e_hbm, e_in)))
    ]
    for load in loads:
        load.start()

    barrier = pltpu.get_barrier_semaphore()

    def tell(devices):
        for device in devices:
            pl.semaphore_signal(barrier, inc=1, device_id=device, device_id_type=MESH)

    tell((from_one, from_two, mate, beyond))

    @pl.when(away)
    def _():
        tell((swap, beside))

    def pack(src, dst, at):
        def body(i, _):
            left, right = packed(src[i])
            dst[at + i, 0:lines] = left
            dst[at + i, lines:] = right
            return 0
        lax.fori_loop(0, SLAB, body, 0)

    def copy(i, src, src_at, dst, dst_at, count, device):
        return pltpu.make_async_remote_copy(
            src_ref=src.at[pl.ds(src_at, count)], dst_ref=dst.at[pl.ds(dst_at, count)],
            send_sem=send_sem.at[i], recv_sem=recv_sem.at[i], device_id=device, device_id_type=MESH,
        )

    def relays(i, buf):
        return (
            copy(i, buf, 4 - core, buf, 7 * core, 3, mate),
            copy(i + 1, buf, 3 + core, buf, 7 * (1 - core), 3, beyond),
        )

    source_one = copy(0, own_s, 0, near_s, 3, SLAB, to_one)
    source_two = copy(1, own_s, 0, next_s, 3, SLAB, to_two)
    target = copy(2, own_t, 0, tgt, 3, SLAB, swap)
    perm = copy(3, eps, 4, eps, 4, SLAB, beside)
    tgt_mate, tgt_beyond = relays(4, tgt)
    near_mate, near_beyond = relays(6, near_s)
    next_mate, next_beyond = relays(8, next_s)
    eps_mate = copy(10, eps, 4, eps, 8 * core, SLAB, mate)
    eps_beyond = copy(11, eps, 4, eps, 8 * (1 - core), SLAB, beyond)

    def result(i):
        return copy(12 + i, done, i, back, i, 1, swap)

    loads[0].wait()
    pack(s_in, own_s, 0)
    loads[1].wait()
    loads[2].wait()

    @pl.when(away)
    def _():
        pack(t_in, own_t, 0)

    @pl.when(home)
    def _():
        pack(t_in, tgt, 3)
        pack(e_in, eps, 4)

    pl.semaphore_wait(barrier, 5)

    def wide_body(i, _):
        left, right = unpacked(eps[i])
        eps_wide[i, :, 0:128] = left
        eps_wide[i, :, 128:WIDE] = right
        return 0

    def coef_body(i, _):
        cells = eps_wide[i + 1]
        ahead_x = 0.5 * (cells + ahead(cells, 0))
        ahead_y = 0.5 * (cells + ahead(cells, 1))
        ahead_z = 0.5 * (cells + eps_wide[i + 2])
        behind_x = behind(ahead_x, 0)
        behind_y = behind(ahead_y, 1)
        behind_z = 0.5 * (cells + eps_wide[i])
        inv = 1.0 / (ahead_x + behind_x + ahead_y + behind_y + ahead_z + behind_z)
        inverse[i] = SCALE * inv
        for j, face in enumerate((ahead_x, behind_x, ahead_y, behind_y, ahead_z, behind_z)):
            coef[j, i] = face * inv
        return 0

    @pl.when(home)
    def _():
        source_one.start()
        perm.start()
        source_two.start()
        eps_mate.start()
        eps_beyond.start()
        tgt_mate.start()
        tgt_beyond.start()

    @pl.when(away)
    def _():
        target.start()
        source_one.start()
        source_two.start()
        perm.wait_recv()
        eps_mate.start()
        eps_beyond.start()
        target.wait_recv()
        tgt_mate.start()
        tgt_beyond.start()

    source_one.wait_recv()
    near_mate.start()
    near_beyond.start()

    eps_mate.wait_recv()
    eps_beyond.wait_recv()
    lax.fori_loop(0, 12, wide_body, 0)
    lax.fori_loop(0, 10, coef_body, 0)

    source_two.wait_recv()
    next_mate.start()
    next_beyond.start()

    def swept(src, i, start):
        cells = src[i]
        near = first[start] + coef[0, start] * ahead(cells, 0) + coef[1, start] * behind(cells, 0)
        near = near + coef[2, start] * ahead(cells, 1) + coef[3, start] * behind(cells, 1)
        return near + coef[4, start] * src[i + 1] + coef[5, start] * src[i - 1]

    def pair(source, last):
        def first_body(i, _):
            left, right = unpacked(source[i] * tgt[i])
            first[i, :, 0:128] = left * inverse[i, :, 0:128]
            first[i, :, 128:WIDE] = right * inverse[i, :, 128:WIDE]
            return 0

        lax.fori_loop(0, 10, first_body, 0)

        def mid_body(i, _):
            mid[i] = swept(first, i + 1, i + 1)
            return 0

        lax.fori_loop(0, 8, mid_body, 0)

        def late_body(i, _):
            late[i] = swept(mid, i + 1, i + 2)
            return 0

        lax.fori_loop(0, 6, late_body, 0)

        def out_body(i, _):
            potential = swept(late, i + 1, i + 3)
            left, right = unpacked(source[3 + i])
            left = left * potential[:, 0:128]
            right = right * potential[:, 128:WIDE]
            if not last:
                total[i, :, 0:128] = left
                total[i, :, 128:WIDE] = right
                return 0
            left = -(total[i, :, 0:128] + left)
            right = -(total[i, :, 128:WIDE] + right)

            @pl.when(home)
            def _():
                out_ref[0, i, :, 0:128] = left
                out_ref[0, i, :, 128:192] = right[:, 0:64]

            @pl.when(away)
            def _():
                done[i, 0:lines] = left
                done[i, lines:] = jnp.concatenate([right[: lines // 2, 0:64], right[lines // 2 :, 0:64]], axis=1)
                result(i).start()
            return 0

        lax.fori_loop(0, SLAB, out_body, 0)

    tgt_mate.wait_recv()
    tgt_beyond.wait_recv()
    near_mate.wait_recv()
    near_beyond.wait_recv()
    pair(near_s, False)
    next_mate.wait_recv()
    next_beyond.wait_recv()
    pair(next_s, True)

    for sent in (source_one, source_two, tgt_mate, tgt_beyond, near_mate, near_beyond, next_mate, next_beyond, eps_mate, eps_beyond):
        sent.wait_send()

    @pl.when(home)
    def _():
        perm.wait_send()

    @pl.when(away)
    def _():
        target.wait_send()

        def back_body(i, _):
            result(i).wait()
            left, right = unpacked(back[i])
            out_ref[0, i, :, 0:128] = left
            out_ref[0, i, :, 128:192] = right[:, 0:64]
            return 0

        lax.fori_loop(0, SLAB, back_body, 0)


def shards(n_blk, n_bulk, targets, sources, permittivity):
    _, planes, lines, cells = targets.shape
    rows = lines * cells // 128

    def plane_stack(count, *tile):
        return pltpu.VMEM((count, *tile), jnp.float32)

    return pl.pallas_call(
        functools.partial(kernel, n_blk, n_bulk),
        out_shape=jax.ShapeDtypeStruct(targets.shape, jnp.float32),
        in_specs=[pl.BlockSpec(memory_space=pl.ANY)] * 3,
        out_specs=pl.BlockSpec(memory_space=pltpu.VMEM),
        scratch_shapes=[
            plane_stack(planes, lines, cells),
            plane_stack(planes, lines, cells),
            plane_stack(planes, lines, cells),
            plane_stack(planes, rows, 128),
            plane_stack(planes, rows, 128),
            plane_stack(10, rows, 128),
            plane_stack(10, rows, 128),
            plane_stack(10, rows, 128),
            plane_stack(12, rows, 128),
            plane_stack(planes, rows, 128),
            plane_stack(planes, rows, 128),
            plane_stack(12, lines, WIDE),
            pltpu.VMEM((6, 10, lines, WIDE), jnp.float32),
            plane_stack(10, lines, WIDE),
            plane_stack(10, lines, WIDE),
            plane_stack(8, lines, WIDE),
            plane_stack(6, lines, WIDE),
            plane_stack(planes, lines, WIDE),
            pltpu.SemaphoreType.DMA((3,)),
            pltpu.SemaphoreType.DMA((16,)),
            pltpu.SemaphoreType.DMA((16,)),
        ],
        compiler_params=pltpu.CompilerParams(collective_id=0, has_side_effects=True, vmem_limit_bytes=60 << 20),
        cost_estimate=pl.CostEstimate(flops=20_000_000, bytes_accessed=1_200_000, transcendentals=0),
    )(targets, sources, permittivity)


def solution(mesh):
    in_specs = (P("blk", "bulk", None, None), P("blk", "bulk", None, None), P("bulk", None, None))
    out_specs = P("blk", "bulk", None, None)
    return jax.shard_map(
        functools.partial(shards, mesh.shape["blk"], mesh.shape["bulk"]),
        mesh=mesh, in_specs=in_specs, out_specs=out_specs, check_vma=False,
    )
```

```python
import functools
import math

import jax
import jax.numpy as jnp
from jax import lax
from jax.experimental import pallas as pl
from jax.experimental.pallas import tpu as pltpu
from jax.sharding import PartitionSpec as P

MESH = pl.DeviceIdType.MESH
SLAB = 4
WIDE = 256
SCALE = math.pi


def packed(plane):
    lines = plane.shape[0]
    right = plane[:, 128:192]
    return plane[:, 0:128], jnp.concatenate([right[: lines // 2], right[lines // 2 :]], axis=1)


def unpacked(both):
    lines = both.shape[0] * 2 // 3
    left, right = both[:lines], both[lines:]
    left_turned = pltpu.roll(left, 64, 1)
    right_turned = pltpu.roll(right, 64, 1)
    lane = lax.broadcasted_iota(jnp.int32, right.shape, 1)
    low = jnp.where(lane < 64, right, jnp.where(lane < 96, left_turned[: lines // 2], right_turned))
    high = jnp.where(lane < 64, right_turned, jnp.where(lane < 96, left_turned[lines // 2 :], right))
    return left, jnp.concatenate([low, high], axis=0)


def each(start, count, body):
    def step(i, carry):
        body(start + i)
        return carry
    lax.fori_loop(0, count, step, 0, unroll=True)


def ahead(cells, axis):
    return pltpu.roll(cells, cells.shape[axis] - 1, axis)


def behind(cells, axis):
    return pltpu.roll(cells, 1, axis)


def kernel(
    n_blk, n_bulk,
    t_hbm, s_hbm, e_hbm, out_ref,
    t_in, s_in, e_in, own_s, own_t, tgt, near_s, next_s, near_rhs, next_rhs, eps, done, back, eps_wide, coef, inverse, first, mid, late, total,
    in_sem, send_sem, recv_sem,
):
    b, k = lax.axis_index("blk"), lax.axis_index("bulk")
    pos, core, z, hi = b // 2, lax.rem(b, 2), k // 2, lax.rem(k, 2)
    n_pos = n_blk // 2
    lines = t_in.shape[1]
    home = core == hi
    away = core != hi
    prev_pos, next_pos = lax.rem(pos + n_pos - 1, n_pos), lax.rem(pos + 1, n_pos)
    mate = (b + 1 - 2 * core, k)
    beyond = (b + 1 - 2 * core, lax.rem(k + n_bulk - 2 + 4 * core, n_bulk))
    swap = (b + 1 - 2 * core, k + 1 - 2 * hi)
    beside = (b + 2 - 4 * lax.rem(pos, 2), k + 1 - 2 * hi)
    to_one = (lax.rem(pos + core, n_pos) * 2 + hi, 2 * z + 1 - core)
    to_two = (next_pos * 2 + hi, 2 * z + core)
    from_one = (lax.rem(pos + n_pos - 1 + hi, n_pos) * 2 + 1 - hi, 2 * z + core)
    from_two = (prev_pos * 2 + hi, 2 * z + core)

    loads = [
        pltpu.make_async_copy(src, dst, in_sem.at[i])
        for i, (src, dst) in enumerate(((s_hbm.at[0], s_in), (t_hbm.at[0], t_in), (e_hbm, e_in)))
    ]
    for load in loads:
        load.start()

    barrier = pltpu.get_barrier_semaphore()

    def tell(devices):
        for device in devices:
            pl.semaphore_signal(barrier, inc=1, device_id=device, device_id_type=MESH)

    tell((from_one, from_two, mate, beyond))

    @pl.when(away)
    def _():
        tell((swap, beside))

    def pack(src, dst, at):
        def body(i):
            left, right = packed(src[i])
            dst[at + i, 0:lines] = left
            dst[at + i, lines:] = right
        each(0, SLAB, body)

    def copy(i, src, src_at, dst, dst_at, count, device, rows=slice(None)):
        return pltpu.make_async_remote_copy(
            src_ref=src.at[pl.ds(src_at, count), rows], dst_ref=dst.at[pl.ds(dst_at, count), rows],
            send_sem=send_sem.at[i], recv_sem=recv_sem.at[i], device_id=device, device_id_type=MESH,
        )

    def relays(i, buf, rows=slice(None)):
        return (
            copy(i, buf, 4 - core, buf, 7 * core, 3, mate, rows),
            copy(i + 1, buf, 3 + core, buf, 7 * (1 - core), 3, beyond, rows),
        )

    half = own_s.shape[1] // 2
    parts = (slice(0, half), slice(half, 2 * half))

    source_one = copy(0, own_s, 0, near_s, 0, SLAB, to_one)
    source_two = [copy(i, own_s, 0, next_s, 0, SLAB, to_two, rows) for i, rows in zip((1, 14), parts)]
    target = copy(2, own_t, 0, tgt, 0, SLAB, swap)
    perm = copy(3, eps, 4, eps, 4, SLAB, beside)
    near_mate, near_beyond = relays(4, near_rhs)
    next_mate, next_beyond = zip(*(relays(i, next_rhs, rows) for i, rows in zip((6, 15), parts)))
    eps_mate = copy(8, eps, 4, eps, 8 * core, SLAB, mate)
    eps_beyond = copy(9, eps, 4, eps, 8 * (1 - core), SLAB, beyond)

    def result(i):
        return copy(10 + i, done, i, back, i, 1, swap)

    loads[0].wait()
    pack(s_in, own_s, 0)
    loads[1].wait()
    loads[2].wait()

    @pl.when(away)
    def _():
        pack(t_in, own_t, 0)

    @pl.when(home)
    def _():
        pack(t_in, tgt, 0)
        pack(e_in, eps, 4)

    pl.semaphore_wait(barrier, 5)

    def wide_body(i):
        left, right = unpacked(eps[i])
        eps_wide[i, :, 0:128] = left
        eps_wide[i, :, 128:WIDE] = right

    def coef_body(i):
        cells = eps_wide[i + 1]
        ahead_x = 0.5 * (cells + ahead(cells, 0))
        ahead_y = 0.5 * (cells + ahead(cells, 1))
        ahead_z = 0.5 * (cells + eps_wide[i + 2])
        behind_x = behind(ahead_x, 0)
        behind_y = behind(ahead_y, 1)
        behind_z = 0.5 * (cells + eps_wide[i])
        inv = 1.0 / (ahead_x + behind_x + ahead_y + behind_y + ahead_z + behind_z)
        inverse[i] = SCALE * inv
        for j, face in enumerate((ahead_x, behind_x, ahead_y, behind_y, ahead_z, behind_z)):
            coef[j, i] = face * inv

    def product(source, rhs, rows=slice(None)):
        def body(i):
            rhs[3 + i, rows] = source[i, rows] * tgt[i, rows]
        each(0, SLAB, body)

    @pl.when(home)
    def _():
        perm.start()
        source_one.start()
        eps_mate.start()
        eps_beyond.start()

    @pl.when(away)
    def _():
        target.start()
        source_one.start()
        perm.wait_recv()
        eps_mate.start()
        eps_beyond.start()
        target.wait_recv()

    source_one.wait_recv()
    source_two[0].start()
    source_two[1].start()
    product(near_s, near_rhs)
    near_mate.start()
    near_beyond.start()

    eps_mate.wait_recv()
    eps_beyond.wait_recv()
    each(0, 12, wide_body)
    each(0, 10, coef_body)

    for i, rows in enumerate(parts):
        source_two[i].wait_recv()
        product(next_s, next_rhs, rows)
        next_mate[i].start()
        next_beyond[i].start()

    def swept(src, i, start):
        cells = src[i]
        near = first[start] + coef[0, start] * ahead(cells, 0) + coef[1, start] * behind(cells, 0)
        near = near + coef[2, start] * ahead(cells, 1) + coef[3, start] * behind(cells, 1)
        return near + coef[4, start] * src[i + 1] + coef[5, start] * src[i - 1]

    def pair(source, rhs, last, from_mate, from_beyond):
        def first_body(i):
            left, right = unpacked(rhs[i])
            first[i, :, 0:128] = left * inverse[i, :, 0:128]
            first[i, :, 128:WIDE] = right * inverse[i, :, 128:WIDE]

        def mid_body(i):
            mid[i] = swept(first, i + 1, i + 1)

        def late_body(i):
            late[i] = swept(mid, i + 1, i + 2)

        def out_body(i):
            potential = swept(late, i + 1, i + 3)
            left, right = unpacked(source[i])
            left = left * potential[:, 0:128]
            right = right * potential[:, 128:WIDE]
            if not last:
                total[i, :, 0:128] = left
                total[i, :, 128:WIDE] = right
                return
            left = -(total[i, :, 0:128] + left)
            right = -(total[i, :, 128:WIDE] + right)
            total[i, :, 0:128] = left
            total[i, :, 128:WIDE] = right

        def hand_over(i):
            left, right = total[i, :, 0:128], total[i, :, 128:WIDE]

            @pl.when(home)
            def _():
                out_ref[0, i, :, 0:128] = left
                out_ref[0, i, :, 128:192] = right[:, 0:64]

            @pl.when(away)
            def _():
                done[i, 0:lines] = left
                done[i, lines:] = jnp.concatenate([right[: lines // 2, 0:64], right[lines // 2 :, 0:64]], axis=1)
                result(i).start()

        for arrival in from_mate:
            arrival.wait_recv()
        each(3 * (1 - core), 7, first_body)
        each(3 * (1 - core), 5, mid_body)
        each(3 * (1 - core), 3, late_body)
        each(3 * (1 - core), 1, out_body)
        if last:
            hand_over(3 * (1 - core))
        for arrival in from_beyond:
            arrival.wait_recv()
        each(7 * core, 3, first_body)
        each(5 * core, 3, mid_body)
        each(3 * core, 3, late_body)
        for i in range(3):
            out_body(core + i)
            if last:
                hand_over(core + i)

    pair(near_s, near_rhs, False, (near_mate,), (near_beyond,))
    pair(next_s, next_rhs, True, next_mate, next_beyond)

    for sent in (source_one, *source_two, near_mate, near_beyond, *next_mate, *next_beyond, eps_mate, eps_beyond):
        sent.wait_send()

    @pl.when(home)
    def _():
        perm.wait_send()

    @pl.when(away)
    def _():
        target.wait_send()

        def back_body(i):
            result(i).wait()
            left, right = unpacked(back[i])
            out_ref[0, i, :, 0:128] = left
            out_ref[0, i, :, 128:192] = right[:, 0:64]

        each(3 * core, 1, back_body)
        each(1 - core, 3, back_body)


def shards(n_blk, n_bulk, targets, sources, permittivity):
    _, planes, lines, cells = targets.shape
    rows = lines * cells // 128

    def plane_stack(count, *tile):
        return pltpu.VMEM((count, *tile), jnp.float32)

    return pl.pallas_call(
        functools.partial(kernel, n_blk, n_bulk),
        out_shape=jax.ShapeDtypeStruct(targets.shape, jnp.float32),
        in_specs=[pl.BlockSpec(memory_space=pl.ANY)] * 3,
        out_specs=pl.BlockSpec(memory_space=pltpu.VMEM),
        scratch_shapes=[
            plane_stack(planes, lines, cells),
            plane_stack(planes, lines, cells),
            plane_stack(planes, lines, cells),
            plane_stack(planes, rows, 128),
            plane_stack(planes, rows, 128),
            plane_stack(planes, rows, 128),
            plane_stack(planes, rows, 128),
            plane_stack(planes, rows, 128),
            plane_stack(10, rows, 128),
            plane_stack(10, rows, 128),
            plane_stack(12, rows, 128),
            plane_stack(planes, rows, 128),
            plane_stack(planes, rows, 128),
            plane_stack(12, lines, WIDE),
            pltpu.VMEM((6, 10, lines, WIDE), jnp.float32),
            plane_stack(10, lines, WIDE),
            plane_stack(10, lines, WIDE),
            plane_stack(8, lines, WIDE),
            plane_stack(6, lines, WIDE),
            plane_stack(planes, lines, WIDE),
            pltpu.SemaphoreType.DMA((3,)),
            pltpu.SemaphoreType.DMA((17,)),
            pltpu.SemaphoreType.DMA((17,)),
        ],
        compiler_params=pltpu.CompilerParams(collective_id=0, has_side_effects=True, vmem_limit_bytes=60 << 20),
        cost_estimate=pl.CostEstimate(flops=20_000_000, bytes_accessed=1_200_000, transcendentals=0),
    )(targets, sources, permittivity)


def solution(mesh):
    in_specs = (P("blk", "bulk", None, None), P("blk", "bulk", None, None), P("bulk", None, None))
    out_specs = P("blk", "bulk", None, None)
    return jax.shard_map(
        functools.partial(shards, mesh.shape["blk"], mesh.shape["bulk"]),
        mesh=mesh, in_specs=in_specs, out_specs=out_specs, check_vma=False,
    )
```

```python
import functools
import math

import jax
import jax.numpy as jnp
from jax import lax
from jax.experimental import pallas as pl
from jax.experimental.pallas import tpu as pltpu
from jax.sharding import PartitionSpec as P

MESH = pl.DeviceIdType.MESH
SLAB = 4
WIDE = 256
SCALE = math.pi


def packed(plane):
    lines = plane.shape[0]
    right = plane[:, 128:192]
    return plane[:, 0:128], jnp.concatenate([right[: lines // 2], right[lines // 2 :]], axis=1)


def unpacked(both):
    lines = both.shape[0] * 2 // 3
    left, right = both[:lines], both[lines:]
    left_turned = pltpu.roll(left, 64, 1)
    right_turned = pltpu.roll(right, 64, 1)
    lane = lax.broadcasted_iota(jnp.int32, right.shape, 1)
    low = jnp.where(lane < 64, right, jnp.where(lane < 96, left_turned[: lines // 2], right_turned))
    high = jnp.where(lane < 64, right_turned, jnp.where(lane < 96, left_turned[lines // 2 :], right))
    return left, jnp.concatenate([low, high], axis=0)


def each(start, count, body):
    def step(i, carry):
        body(start + i)
        return carry
    lax.fori_loop(0, count, step, 0, unroll=True)


def ahead(cells, axis):
    return pltpu.roll(cells, cells.shape[axis] - 1, axis)


def behind(cells, axis):
    return pltpu.roll(cells, 1, axis)


def kernel(
    n_blk, n_bulk,
    t_hbm, s_hbm, e_hbm, out_ref,
    t_in, s_in, e_in, own_s, own_t, tgt, near_s, next_s, near_rhs, next_rhs, eps, done, back, eps_wide, coef, inverse, first, mid, late, total,
    in_sem, send_sem, recv_sem,
):
    b, k = lax.axis_index("blk"), lax.axis_index("bulk")
    pos, core, z, hi = b // 2, lax.rem(b, 2), k // 2, lax.rem(k, 2)
    n_pos = n_blk // 2
    lines = t_in.shape[1]
    home = core == hi
    away = core != hi
    prev_pos, next_pos = lax.rem(pos + n_pos - 1, n_pos), lax.rem(pos + 1, n_pos)
    mate = (b + 1 - 2 * core, k)
    beyond = (b + 1 - 2 * core, lax.rem(k + n_bulk - 2 + 4 * core, n_bulk))
    swap = (b + 1 - 2 * core, k + 1 - 2 * hi)
    beside = (b + 2 - 4 * lax.rem(pos, 2), k + 1 - 2 * hi)
    to_one = (lax.rem(pos + core, n_pos) * 2 + hi, 2 * z + 1 - core)
    to_two = (next_pos * 2 + hi, 2 * z + core)
    from_one = (lax.rem(pos + n_pos - 1 + hi, n_pos) * 2 + 1 - hi, 2 * z + core)
    from_two = (prev_pos * 2 + hi, 2 * z + core)

    loads = [
        pltpu.make_async_copy(src, dst, in_sem.at[i])
        for i, (src, dst) in enumerate(((s_hbm.at[0], s_in), (t_hbm.at[0], t_in), (e_hbm, e_in)))
    ]
    for load in loads:
        load.start()

    barrier = pltpu.get_barrier_semaphore()

    def tell(devices):
        for device in devices:
            pl.semaphore_signal(barrier, inc=1, device_id=device, device_id_type=MESH)

    tell((from_one, from_two, mate, beyond))

    @pl.when(away)
    def _():
        tell((swap, beside))

    def pack(src, dst, at):
        def body(i):
            left, right = packed(src[i])
            dst[at + i, 0:lines] = left
            dst[at + i, lines:] = right
        each(0, SLAB, body)

    def copy(i, src, src_at, dst, dst_at, count, device, rows=slice(None)):
        return pltpu.make_async_remote_copy(
            src_ref=src.at[pl.ds(src_at, count), rows], dst_ref=dst.at[pl.ds(dst_at, count), rows],
            send_sem=send_sem.at[i], recv_sem=recv_sem.at[i], device_id=device, device_id_type=MESH,
        )

    def relays(i, buf, rows=slice(None)):
        return (
            copy(i, buf, 4 - core, buf, 7 * core, 3, mate, rows),
            copy(i + 1, buf, 3 + core, buf, 7 * (1 - core), 3, beyond, rows),
        )

    half = own_s.shape[1] // 2
    parts = (slice(0, half), slice(half, 2 * half))

    source_one = copy(0, own_s, 0, near_s, 0, SLAB, to_one)
    source_two = [copy(i, own_s, 0, next_s, 0, SLAB, to_two, rows) for i, rows in zip((1, 14), parts)]
    target = copy(2, own_t, 0, tgt, 0, SLAB, swap)
    perm = copy(3, eps, 4, eps, 4, SLAB, beside)
    near_mate, near_beyond = relays(4, near_rhs)
    next_mate, next_beyond = zip(*(relays(i, next_rhs, rows) for i, rows in zip((6, 15), parts)))
    eps_mate = copy(8, eps, 4, eps, 8 * core, SLAB, mate)
    eps_beyond = copy(9, eps, 4, eps, 8 * (1 - core), SLAB, beyond)

    def result(i):
        return copy(10 + i, done, i, back, i, 1, swap)

    loads[0].wait()
    pack(s_in, own_s, 0)
    loads[1].wait()
    loads[2].wait()

    @pl.when(away)
    def _():
        pack(t_in, own_t, 0)

    @pl.when(home)
    def _():
        pack(t_in, tgt, 0)
        pack(e_in, eps, 4)

    pl.semaphore_wait(barrier, 5)

    def wide_body(i):
        left, right = unpacked(eps[i])
        eps_wide[i, :, 0:128] = left
        eps_wide[i, :, 128:WIDE] = right

    def coef_body(i):
        cells = eps_wide[i + 1]
        ahead_x = 0.5 * (cells + ahead(cells, 0))
        ahead_y = 0.5 * (cells + ahead(cells, 1))
        ahead_z = 0.5 * (cells + eps_wide[i + 2])
        behind_x = behind(ahead_x, 0)
        behind_y = behind(ahead_y, 1)
        behind_z = 0.5 * (cells + eps_wide[i])
        inv = 1.0 / (ahead_x + behind_x + ahead_y + behind_y + ahead_z + behind_z)
        inverse[i] = SCALE * inv
        for j, face in enumerate((ahead_x, behind_x, ahead_y, behind_y, ahead_z, behind_z)):
            coef[j, i] = face * inv

    def product(source, rhs, rows=slice(None)):
        def body(i):
            rhs[3 + i, rows] = source[i, rows] * tgt[i, rows]
        each(0, SLAB, body)

    @pl.when(home)
    def _():
        perm.start()
        source_one.start()
        eps_mate.start()
        eps_beyond.start()

    @pl.when(away)
    def _():
        source_one.start()
        target.start()
        perm.wait_recv()
        eps_mate.start()
        eps_beyond.start()
        target.wait_recv()

    source_one.wait_recv()
    source_two[0].start()
    source_two[1].start()
    product(near_s, near_rhs)
    near_mate.start()
    near_beyond.start()

    eps_mate.wait_recv()
    each(4 * (1 - core), 8, wide_body)
    each(4 * (1 - core), 6, coef_body)

    for i, rows in enumerate(parts):
        source_two[i].wait_recv()
        product(next_s, next_rhs, rows)
        next_mate[i].start()
        next_beyond[i].start()

    def swept(j, src, i, start):
        cells = src[j, i]
        near = first[j, start] + coef[0, start] * ahead(cells, 0) + coef[1, start] * behind(cells, 0)
        near = near + coef[2, start] * ahead(cells, 1) + coef[3, start] * behind(cells, 1)
        return near + coef[4, start] * src[j, i + 1] + coef[5, start] * src[j, i - 1]

    def first_body(j, rhs, i):
        left, right = unpacked(rhs[i])
        first[j, i, :, 0:128] = left * inverse[i, :, 0:128]
        first[j, i, :, 128:WIDE] = right * inverse[i, :, 128:WIDE]

    def mid_body(j, i):
        mid[j, i] = swept(j, first, i + 1, i + 1)

    def late_body(j, i):
        late[j, i] = swept(j, mid, i + 1, i + 2)

    def weighted(j, source, i):
        potential = swept(j, late, i + 1, i + 3)
        left, right = unpacked(source[i])
        return left * potential[:, 0:128], right * potential[:, 128:WIDE]

    def sooner(j, rhs, arrivals):
        for arrival in arrivals:
            arrival.wait_recv()
        each(4 * (1 - core), 6, functools.partial(first_body, j, rhs))
        each(4 * (1 - core), 4, functools.partial(mid_body, j))
        each(4 * (1 - core), 2, functools.partial(late_body, j))

    def later(j, rhs, arrivals):
        for arrival in arrivals:
            arrival.wait_recv()
        each(6 * core, 4, functools.partial(first_body, j, rhs))
        each(4 * core, 4, functools.partial(mid_body, j))
        each(2 * core, 4, functools.partial(late_body, j))

    def near_out(i):
        total[i, :, 0:128], total[i, :, 128:WIDE] = weighted(0, near_s, i)

    def hand_over(i):
        left, right = weighted(1, next_s, i)
        left = -(total[i, :, 0:128] + left)
        right = -(total[i, :, 128:WIDE] + right)

        @pl.when(home)
        def _():
            out_ref[0, i, :, 0:128] = left
            out_ref[0, i, :, 128:192] = right[:, 0:64]

        @pl.when(away)
        def _():
            done[i, 0:lines] = left
            done[i, lines:] = jnp.concatenate([right[: lines // 2, 0:64], right[lines // 2 :, 0:64]], axis=1)
            result(i).start()

    sooner(0, near_rhs, (near_mate,))
    sooner(1, next_rhs, next_mate)
    eps_beyond.wait_recv()
    each(8 * core, 4, wide_body)
    each(6 * core, 4, coef_body)
    later(0, near_rhs, (near_beyond,))
    each(0, SLAB, near_out)
    later(1, next_rhs, next_beyond)
    for i in range(SLAB):
        hand_over(i)

    for sent in (source_one, *source_two, near_mate, near_beyond, *next_mate, *next_beyond, eps_mate, eps_beyond):
        sent.wait_send()

    @pl.when(home)
    def _():
        perm.wait_send()

    @pl.when(away)
    def _():
        target.wait_send()

        def back_body(i):
            result(i).wait()
            left, right = unpacked(back[i])
            out_ref[0, i, :, 0:128] = left
            out_ref[0, i, :, 128:192] = right[:, 0:64]

        each(0, SLAB, back_body)


def shards(n_blk, n_bulk, targets, sources, permittivity):
    _, planes, lines, cells = targets.shape
    rows = lines * cells // 128

    def plane_stack(count, *tile):
        return pltpu.VMEM((count, *tile), jnp.float32)

    return pl.pallas_call(
        functools.partial(kernel, n_blk, n_bulk),
        out_shape=jax.ShapeDtypeStruct(targets.shape, jnp.float32),
        in_specs=[pl.BlockSpec(memory_space=pl.ANY)] * 3,
        out_specs=pl.BlockSpec(memory_space=pltpu.VMEM),
        scratch_shapes=[
            plane_stack(planes, lines, cells),
            plane_stack(planes, lines, cells),
            plane_stack(planes, lines, cells),
            plane_stack(planes, rows, 128),
            plane_stack(planes, rows, 128),
            plane_stack(planes, rows, 128),
            plane_stack(planes, rows, 128),
            plane_stack(planes, rows, 128),
            plane_stack(10, rows, 128),
            plane_stack(10, rows, 128),
            plane_stack(12, rows, 128),
            plane_stack(planes, rows, 128),
            plane_stack(planes, rows, 128),
            plane_stack(12, lines, WIDE),
            pltpu.VMEM((6, 10, lines, WIDE), jnp.float32),
            plane_stack(10, lines, WIDE),
            pltpu.VMEM((2, 10, lines, WIDE), jnp.float32),
            pltpu.VMEM((2, 8, lines, WIDE), jnp.float32),
            pltpu.VMEM((2, 6, lines, WIDE), jnp.float32),
            plane_stack(planes, lines, WIDE),
            pltpu.SemaphoreType.DMA((3,)),
            pltpu.SemaphoreType.DMA((17,)),
            pltpu.SemaphoreType.DMA((17,)),
        ],
        compiler_params=pltpu.CompilerParams(collective_id=0, has_side_effects=True, vmem_limit_bytes=60 << 20),
        cost_estimate=pl.CostEstimate(flops=20_000_000, bytes_accessed=1_200_000, transcendentals=0),
    )(targets, sources, permittivity)


def solution(mesh):
    in_specs = (P("blk", "bulk", None, None), P("blk", "bulk", None, None), P("bulk", None, None))
    out_specs = P("blk", "bulk", None, None)
    return jax.shard_map(
        functools.partial(shards, mesh.shape["blk"], mesh.shape["bulk"]),
        mesh=mesh, in_specs=in_specs, out_specs=out_specs, check_vma=False,
    )
```

```python
import functools
import math

import jax
import jax.numpy as jnp
from jax import lax
from jax.experimental import pallas as pl
from jax.experimental.pallas import tpu as pltpu
from jax.sharding import PartitionSpec as P

MESH = pl.DeviceIdType.MESH
SLAB = 4
WIDE = 256
SCALE = math.pi


def packed(plane):
    lines = plane.shape[0]
    right = plane[:, 128:192]
    return plane[:, 0:128], jnp.concatenate([right[: lines // 2], right[lines // 2 :]], axis=1)


def unpacked(both):
    lines = both.shape[0] * 2 // 3
    left, right = both[:lines], both[lines:]
    left_turned = pltpu.roll(left, 64, 1)
    right_turned = pltpu.roll(right, 64, 1)
    lane = lax.broadcasted_iota(jnp.int32, right.shape, 1)
    low = jnp.where(lane < 64, right, jnp.where(lane < 96, left_turned[: lines // 2], right_turned))
    high = jnp.where(lane < 64, right_turned, jnp.where(lane < 96, left_turned[lines // 2 :], right))
    return left, jnp.concatenate([low, high], axis=0)


def each(start, count, body):
    def step(i, carry):
        body(start + i)
        return carry
    lax.fori_loop(0, count, step, 0, unroll=True)


def ahead(cells, axis):
    return pltpu.roll(cells, cells.shape[axis] - 1, axis)


def behind(cells, axis):
    return pltpu.roll(cells, 1, axis)


def kernel(
    n_blk, n_bulk,
    t_hbm, s_hbm, e_hbm, out_ref,
    t_in, s_in, e_in, own_s, own_t, tgt, near_s, next_s, near_rhs, next_rhs, eps, done, back, eps_wide, coef, inverse, first, mid, late, total,
    in_sem, send_sem, recv_sem,
):
    b, k = lax.axis_index("blk"), lax.axis_index("bulk")
    pos, core, z, hi = b // 2, lax.rem(b, 2), k // 2, lax.rem(k, 2)
    n_pos = n_blk // 2
    lines = t_in.shape[1]
    home = core == hi
    away = core != hi
    prev_pos, next_pos = lax.rem(pos + n_pos - 1, n_pos), lax.rem(pos + 1, n_pos)
    mate = (b + 1 - 2 * core, k)
    beyond = (b + 1 - 2 * core, lax.rem(k + n_bulk - 2 + 4 * core, n_bulk))
    swap = (b + 1 - 2 * core, k + 1 - 2 * hi)
    beside = (b + 2 - 4 * lax.rem(pos, 2), k + 1 - 2 * hi)
    to_one = (lax.rem(pos + core, n_pos) * 2 + hi, 2 * z + 1 - core)
    to_two = (next_pos * 2 + hi, 2 * z + core)
    from_one = (lax.rem(pos + n_pos - 1 + hi, n_pos) * 2 + 1 - hi, 2 * z + core)
    from_two = (prev_pos * 2 + hi, 2 * z + core)

    loads = [
        pltpu.make_async_copy(src, dst, in_sem.at[i])
        for i, (src, dst) in enumerate(((s_hbm.at[0], s_in), (t_hbm.at[0], t_in), (e_hbm, e_in)))
    ]
    for load in loads:
        load.start()

    barrier = pltpu.get_barrier_semaphore()

    def tell(devices):
        for device in devices:
            pl.semaphore_signal(barrier, inc=1, device_id=device, device_id_type=MESH)

    tell((from_one, from_two, mate, beyond))

    @pl.when(away)
    def _():
        tell((swap, beside))

    def pack(src, dst, at):
        def body(i):
            left, right = packed(src[i])
            dst[at + i, 0:lines] = left
            dst[at + i, lines:] = right
        each(0, SLAB, body)

    def copy(i, src, src_at, dst, dst_at, count, device, rows=slice(None)):
        return pltpu.make_async_remote_copy(
            src_ref=src.at[pl.ds(src_at, count), rows], dst_ref=dst.at[pl.ds(dst_at, count), rows],
            send_sem=send_sem.at[i], recv_sem=recv_sem.at[i], device_id=device, device_id_type=MESH,
        )

    def relays(i, buf, rows=slice(None)):
        return (
            copy(i, buf, 4 - core, buf, 7 * core, 3, mate, rows),
            copy(i + 1, buf, 3 + core, buf, 7 * (1 - core), 3, beyond, rows),
        )

    half = own_s.shape[1] // 2
    parts = (slice(0, half), slice(half, 2 * half))

    source_one = copy(0, own_s, 0, near_s, 0, SLAB, to_one)
    source_two = [copy(i, own_s, 0, next_s, 0, SLAB, to_two, rows) for i, rows in zip((1, 14), parts)]
    target = copy(2, own_t, 0, tgt, 0, SLAB, swap)
    perm = copy(3, eps, 4, eps, 4, SLAB, beside)
    near_mate, near_beyond = relays(4, near_rhs)
    next_mate, next_beyond = zip(*(relays(i, next_rhs, rows) for i, rows in zip((6, 15), parts)))
    eps_mate = copy(8, eps, 4, eps, 8 * core, SLAB, mate)
    eps_beyond = copy(9, eps, 4, eps, 8 * (1 - core), SLAB, beyond)

    def result(i):
        return copy(10 + i, done, i, back, i, 1, swap)

    loads[0].wait()
    pack(s_in, own_s, 0)
    loads[1].wait()
    loads[2].wait()

    @pl.when(away)
    def _():
        pack(t_in, own_t, 0)

    @pl.when(home)
    def _():
        pack(t_in, tgt, 0)
        pack(e_in, eps, 4)

    pl.semaphore_wait(barrier, 5)

    def wide_body(i):
        left, right = unpacked(eps[i])
        eps_wide[i, :, 0:128] = left
        eps_wide[i, :, 128:WIDE] = right

    def coef_body(i):
        cells = eps_wide[i + 1]
        ahead_x = 0.5 * (cells + ahead(cells, 0))
        ahead_y = 0.5 * (cells + ahead(cells, 1))
        ahead_z = 0.5 * (cells + eps_wide[i + 2])
        behind_x = behind(ahead_x, 0)
        behind_y = behind(ahead_y, 1)
        behind_z = 0.5 * (cells + eps_wide[i])
        inv = 1.0 / (ahead_x + behind_x + ahead_y + behind_y + ahead_z + behind_z)
        inverse[i] = SCALE * inv
        for j, face in enumerate((ahead_x, behind_x, ahead_y, behind_y, ahead_z, behind_z)):
            coef[j, i] = face * inv

    def product(source, rhs, rows=slice(None)):
        def body(i):
            rhs[3 + i, rows] = source[i, rows] * tgt[i, rows]
        each(0, SLAB, body)

    @pl.when(home)
    def _():
        perm.start()
        source_one.start()
        eps_mate.start()
        eps_beyond.start()

    @pl.when(away)
    def _():
        source_one.start()
        target.start()
        perm.wait_recv()
        eps_mate.start()
        eps_beyond.start()
        target.wait_recv()

    source_one.wait_recv()
    source_two[0].start()
    source_two[1].start()
    product(near_s, near_rhs)
    near_mate.start()
    near_beyond.start()

    eps_mate.wait_recv()
    each(4 * (1 - core), 8, wide_body)
    each(4 * (1 - core), 6, coef_body)

    for i, rows in enumerate(parts):
        source_two[i].wait_recv()
        product(next_s, next_rhs, rows)
        next_mate[i].start()
        next_beyond[i].start()

    def swept(j, src, i, start):
        cells = src[j, i]
        near = first[j, start] + coef[0, start] * ahead(cells, 0) + coef[1, start] * behind(cells, 0)
        near = near + coef[2, start] * ahead(cells, 1) + coef[3, start] * behind(cells, 1)
        return near + coef[4, start] * src[j, i + 1] + coef[5, start] * src[j, i - 1]

    def first_body(j, rhs, i):
        left, right = unpacked(rhs[i])
        first[j, i, :, 0:128] = left * inverse[i, :, 0:128]
        first[j, i, :, 128:WIDE] = right * inverse[i, :, 128:WIDE]

    def mid_body(j, i):
        mid[j, i] = swept(j, first, i + 1, i + 1)

    def late_body(j, i):
        late[j, i] = swept(j, mid, i + 1, i + 2)

    def weighted(j, source, i):
        potential = swept(j, late, i + 1, i + 3)
        left, right = unpacked(source[i])
        return left * potential[:, 0:128], right * potential[:, 128:WIDE]

    def sooner(j, rhs, arrivals):
        for arrival in arrivals:
            arrival.wait_recv()
        each(4 * (1 - core), 6, functools.partial(first_body, j, rhs))
        each(4 * (1 - core), 4, functools.partial(mid_body, j))
        each(4 * (1 - core), 2, functools.partial(late_body, j))

    def later(j, rhs, arrivals):
        for arrival in arrivals:
            arrival.wait_recv()
        each(6 * core, 4, functools.partial(first_body, j, rhs))
        each(4 * core, 4, functools.partial(mid_body, j))
        each(2 * core, 4, functools.partial(late_body, j))

    def near_out(i):
        total[i, :, 0:128], total[i, :, 128:WIDE] = weighted(0, near_s, i)

    def hand_over(i):
        left, right = weighted(1, next_s, i)
        left = -(total[i, :, 0:128] + left)
        right = -(total[i, :, 128:WIDE] + right)

        @pl.when(home)
        def _():
            out_ref[0, i, :, 0:128] = left
            out_ref[0, i, :, 128:192] = right[:, 0:64]

        @pl.when(away)
        def _():
            done[i, 0:lines] = left
            done[i, lines:] = jnp.concatenate([right[: lines // 2, 0:64], right[lines // 2 :, 0:64]], axis=1)
            result(i).start()

    sooner(0, near_rhs, (near_mate,))
    sooner(1, next_rhs, next_mate)
    eps_beyond.wait_recv()
    each(8 * core, 4, wide_body)
    each(6 * core, 4, coef_body)
    later(0, near_rhs, (near_beyond,))
    each(0, SLAB, near_out)
    later(1, next_rhs, next_beyond)
    for i in range(SLAB):
        hand_over(i)

    for sent in (source_one, *source_two, near_mate, near_beyond, *next_mate, *next_beyond, eps_mate, eps_beyond):
        sent.wait_send()

    @pl.when(home)
    def _():
        perm.wait_send()

    @pl.when(away)
    def _():
        target.wait_send()

        def back_body(i):
            result(i).wait()
            left, right = unpacked(back[i])
            out_ref[0, i, :, 0:128] = left
            out_ref[0, i, :, 128:192] = right[:, 0:64]

        each(0, SLAB, back_body)


def shards(n_blk, n_bulk, targets, sources, permittivity):
    _, planes, lines, cells = targets.shape
    rows = lines * cells // 128

    def plane_stack(count, *tile):
        return pltpu.VMEM((count, *tile), jnp.float32)

    return pl.pallas_call(
        functools.partial(kernel, n_blk, n_bulk),
        out_shape=jax.ShapeDtypeStruct(targets.shape, jnp.float32),
        in_specs=[pl.BlockSpec(memory_space=pl.ANY)] * 3,
        out_specs=pl.BlockSpec(memory_space=pltpu.VMEM),
        scratch_shapes=[
            plane_stack(planes, lines, cells),
            plane_stack(planes, lines, cells),
            plane_stack(planes, lines, cells),
            plane_stack(planes, rows, 128),
            plane_stack(planes, rows, 128),
            plane_stack(planes, rows, 128),
            plane_stack(planes, rows, 128),
            plane_stack(planes, rows, 128),
            plane_stack(10, rows, 128),
            plane_stack(10, rows, 128),
            plane_stack(12, rows, 128),
            plane_stack(planes, rows, 128),
            plane_stack(planes, rows, 128),
            plane_stack(12, lines, WIDE),
            pltpu.VMEM((6, 10, lines, WIDE), jnp.float32),
            plane_stack(10, lines, WIDE),
            pltpu.VMEM((2, 10, lines, WIDE), jnp.float32),
            pltpu.VMEM((2, 8, lines, WIDE), jnp.float32),
            pltpu.VMEM((2, 6, lines, WIDE), jnp.float32),
            plane_stack(planes, lines, WIDE),
            pltpu.SemaphoreType.DMA((3,)),
            pltpu.SemaphoreType.DMA((17,)),
            pltpu.SemaphoreType.DMA((17,)),
        ],
        compiler_params=pltpu.CompilerParams(collective_id=0, has_side_effects=True, vmem_limit_bytes=(53 << 20) + (3 << 17)),
        cost_estimate=pl.CostEstimate(flops=20_000_000, bytes_accessed=1_200_000, transcendentals=0),
    )(targets, sources, permittivity)


def solution(mesh):
    in_specs = (P("blk", "bulk", None, None), P("blk", "bulk", None, None), P("bulk", None, None))
    out_specs = P("blk", "bulk", None, None)
    return jax.shard_map(
        functools.partial(shards, mesh.shape["blk"], mesh.shape["bulk"]),
        mesh=mesh, in_specs=in_specs, out_specs=out_specs, check_vma=False,
    )
```

```python
import functools
import math

import jax
import jax.numpy as jnp
from jax import lax
from jax.experimental import pallas as pl
from jax.experimental.pallas import tpu as pltpu
from jax.sharding import PartitionSpec as P

MESH = pl.DeviceIdType.MESH
SLAB = 4
WIDE = 256
SCALE = math.pi


def packed(plane):
    lines = plane.shape[0]
    right = plane[:, 128:192]
    return plane[:, 0:128], jnp.concatenate([right[: lines // 2], right[lines // 2 :]], axis=1)


def unpacked(both):
    lines = both.shape[0] * 2 // 3
    left, right = both[:lines], both[lines:]
    left_turned = pltpu.roll(left, 64, 1)
    right_turned = pltpu.roll(right, 64, 1)
    lane = lax.broadcasted_iota(jnp.int32, right.shape, 1)
    low = jnp.where(lane < 64, right, jnp.where(lane < 96, left_turned[: lines // 2], right_turned))
    high = jnp.where(lane < 64, right_turned, jnp.where(lane < 96, left_turned[lines // 2 :], right))
    return left, jnp.concatenate([low, high], axis=0)


def each(start, count, body):
    def step(i, carry):
        body(start + i)
        return carry
    lax.fori_loop(0, count, step, 0, unroll=True)


def ahead(cells, axis):
    return pltpu.roll(cells, cells.shape[axis] - 1, axis)


def behind(cells, axis):
    return pltpu.roll(cells, 1, axis)


def kernel(
    n_blk, n_bulk,
    t_hbm, s_hbm, e_hbm, out_ref,
    t_in, s_in, e_in, own_s, own_t, tgt, near_s, next_s, near_rhs, next_rhs, eps, done, back, eps_wide, coef, inverse, first, mid, late, total,
    in_sem, send_sem, recv_sem,
):
    b, k = lax.axis_index("blk"), lax.axis_index("bulk")
    pos, core, z, hi = b // 2, lax.rem(b, 2), k // 2, lax.rem(k, 2)
    n_pos, n_z = n_blk // 2, n_bulk // 2
    lines = t_in.shape[1]

    def worker(at, which, layer, side):
        return at * 2 + 1 - side, 2 * layer + 1 - which

    side, which = 1 - core, 1 - hi
    home = side == hi
    away = side != hi
    prev_pos, next_pos = lax.rem(pos + n_pos - 1, n_pos), lax.rem(pos + 1, n_pos)
    mate = (b + 1 - 2 * core, k)
    beyond = (b + 1 - 2 * core, lax.rem(z + n_z - 1 + 2 * side, n_z) * 2 + hi)
    swap = (b + 1 - 2 * core, k + 1 - 2 * hi)
    beside = (b + 2 - 4 * lax.rem(pos, 2), k + 1 - 2 * hi)
    n_x = n_blk // 4
    share = SLAB // n_x
    alike = [(lax.rem(b + 4 * j, n_blk), k) for j in range(n_x)]
    to_one = worker(lax.rem(pos + core, n_pos), 1 - core, z, hi)
    to_two = worker(next_pos, core, z, hi)
    from_one = (lax.rem(pos + n_pos - 1 + which, n_pos) * 2 + 1 - which, 2 * z + side)
    from_two = (prev_pos * 2 + which, 2 * z + side)

    loads = [
        pltpu.make_async_copy(src, dst, in_sem.at[i])
        for i, (src, dst) in enumerate(((s_hbm.at[0], s_in), (t_hbm.at[0], t_in), (e_hbm, e_in)))
    ]
    for load in loads:
        load.start()

    barrier = pltpu.get_barrier_semaphore()

    def tell(devices):
        for device in devices:
            pl.semaphore_signal(barrier, inc=1, device_id=device, device_id_type=MESH)

    tell((from_one, from_two, mate, beyond))

    @pl.when(away)
    def _():
        tell((swap, beside))

    def pack(src, dst, at):
        def body(i):
            left, right = packed(src[i])
            dst[at + i, 0:lines] = left
            dst[at + i, lines:] = right
        each(0, SLAB, body)

    def copy(i, src, src_at, dst, dst_at, count, device, rows=slice(None)):
        return pltpu.make_async_remote_copy(
            src_ref=src.at[pl.ds(src_at, count), rows], dst_ref=dst.at[pl.ds(dst_at, count), rows],
            send_sem=send_sem.at[i], recv_sem=recv_sem.at[i], device_id=device, device_id_type=MESH,
        )

    def relays(i, buf, rows=slice(None)):
        return (
            copy(i, buf, 4 - side, buf, 7 * side, 3, mate, rows),
            copy(i + 1, buf, 3 + side, buf, 7 * (1 - side), 3, beyond, rows),
        )

    half = own_s.shape[1] // 2
    parts = (slice(0, half), slice(half, 2 * half))

    source_one = copy(0, own_s, 0, near_s, 0, SLAB, to_one)
    source_two = [copy(i, own_s, 0, next_s, 0, SLAB, to_two, rows) for i, rows in zip((1, 14), parts)]
    target = copy(2, own_t, 0, tgt, 0, SLAB, swap)
    perm = copy(3, eps, 4, eps, 4, SLAB, beside)
    near_mate, near_beyond = relays(4, near_rhs)
    next_mate, next_beyond = zip(*(relays(i, next_rhs, rows) for i, rows in zip((6, 15), parts)))
    eps_mate = copy(8, eps, 4, eps, 8 * side, SLAB, mate)
    eps_beyond = copy(9, eps, 4, eps, 8 * (1 - side), SLAB, beyond)

    def result(i):
        return copy(10 + i, done, i, back, i, 1, swap)

    loads[0].wait()
    pack(s_in, own_s, 0)
    loads[1].wait()
    loads[2].wait()

    @pl.when(away)
    def _():
        pack(t_in, own_t, 0)

    @pl.when(home)
    def _():
        pack(t_in, tgt, 0)
        pack(e_in, eps, 4)

    pl.semaphore_wait(barrier, 5)

    def wide_body(i):
        left, right = unpacked(eps[i])
        eps_wide[i, :, 0:128] = left
        eps_wide[i, :, 128:WIDE] = right

    def coef_body(i):
        cells = eps_wide[i + 1]
        ahead_x = 0.5 * (cells + ahead(cells, 0))
        ahead_y = 0.5 * (cells + ahead(cells, 1))
        ahead_z = 0.5 * (cells + eps_wide[i + 2])
        behind_x = behind(ahead_x, 0)
        behind_y = behind(ahead_y, 1)
        behind_z = 0.5 * (cells + eps_wide[i])
        inv = 1.0 / (ahead_x + behind_x + ahead_y + behind_y + ahead_z + behind_z)
        inverse[i] = SCALE * inv
        for j, face in enumerate((ahead_x, behind_x, ahead_y, behind_y, ahead_z, behind_z)):
            coef[j, i] = face * inv

    def product(source, rhs, rows=slice(None)):
        def body(i):
            rhs[3 + i, rows] = source[i, rows] * tgt[i, rows]
        each(0, SLAB, body)

    @pl.when(home)
    def _():
        perm.start()
        source_one.start()
        eps_mate.start()
        eps_beyond.start()

    @pl.when(away)
    def _():
        source_one.start()
        target.start()
        perm.wait_recv()
        eps_mate.start()
        eps_beyond.start()
        target.wait_recv()

    source_one.wait_recv()
    source_two[0].start()
    source_two[1].start()
    product(near_s, near_rhs)
    near_mate.start()
    near_beyond.start()

    eps_mate.wait_recv()
    each(4 * (1 - side), 8, wide_body)
    each(4 * (1 - side), 6, coef_body)

    for i, rows in enumerate(parts):
        source_two[i].wait_recv()
        product(next_s, next_rhs, rows)
        next_mate[i].start()
        next_beyond[i].start()

    def swept(j, src, i, start):
        cells = src[j, i]
        near = first[j, start] + coef[0, start] * ahead(cells, 0) + coef[1, start] * behind(cells, 0)
        near = near + coef[2, start] * ahead(cells, 1) + coef[3, start] * behind(cells, 1)
        return near + coef[4, start] * src[j, i + 1] + coef[5, start] * src[j, i - 1]

    def first_body(j, rhs, i):
        left, right = unpacked(rhs[i])
        first[j, i, :, 0:128] = left * inverse[i, :, 0:128]
        first[j, i, :, 128:WIDE] = right * inverse[i, :, 128:WIDE]

    def mid_body(j, i):
        mid[j, i] = swept(j, first, i + 1, i + 1)

    def late_body(j, i):
        late[j, i] = swept(j, mid, i + 1, i + 2)

    def weighted(j, source, i):
        potential = swept(j, late, i + 1, i + 3)
        left, right = unpacked(source[i])
        return left * potential[:, 0:128], right * potential[:, 128:WIDE]

    def sooner(j, rhs, arrivals):
        for arrival in arrivals:
            arrival.wait_recv()
        each(4 * (1 - side), 6, functools.partial(first_body, j, rhs))
        each(4 * (1 - side), 4, functools.partial(mid_body, j))
        each(4 * (1 - side), 2, functools.partial(late_body, j))

    def later(j, rhs, arrivals):
        for arrival in arrivals:
            arrival.wait_recv()
        each(6 * side, 4, functools.partial(first_body, j, rhs))
        each(4 * side, 4, functools.partial(mid_body, j))
        each(2 * side, 4, functools.partial(late_body, j))

    def near_out(i):
        total[i, :, 0:128], total[i, :, 128:WIDE] = weighted(0, near_s, i)

    def hand_over(i):
        left, right = weighted(1, next_s, i)
        left = -(total[i, :, 0:128] + left)
        right = -(total[i, :, 128:WIDE] + right)

        @pl.when(home)
        def _():
            out_ref[0, i, :, 0:128] = left
            out_ref[0, i, :, 128:192] = right[:, 0:64]

        @pl.when(away)
        def _():
            done[i, 0:lines] = left
            done[i, lines:] = jnp.concatenate([right[: lines // 2, 0:64], right[lines // 2 :, 0:64]], axis=1)
            result(i).start()

    sooner(0, near_rhs, (near_mate,))
    sooner(1, next_rhs, next_mate)
    eps_beyond.wait_recv()
    each(8 * side, 4, wide_body)
    each(6 * side, 4, coef_body)
    later(0, near_rhs, (near_beyond,))
    each(0, SLAB, near_out)
    later(1, next_rhs, next_beyond)
    for i in range(SLAB):
        hand_over(i)

    for sent in (source_one, *source_two, near_mate, near_beyond, *next_mate, *next_beyond, eps_mate, eps_beyond):
        sent.wait_send()

    @pl.when(home)
    def _():
        perm.wait_send()

    @pl.when(away)
    def _():
        target.wait_send()

        def back_body(i):
            result(i).wait()
            left, right = unpacked(back[i])
            out_ref[0, i, :, 0:128] = left
            out_ref[0, i, :, 128:192] = right[:, 0:64]

        each(0, SLAB, back_body)


def shards(n_blk, n_bulk, targets, sources, permittivity):
    _, planes, lines, cells = targets.shape
    rows = lines * cells // 128

    def plane_stack(count, *tile):
        return pltpu.VMEM((count, *tile), jnp.float32)

    return pl.pallas_call(
        functools.partial(kernel, n_blk, n_bulk),
        out_shape=jax.ShapeDtypeStruct(targets.shape, jnp.float32),
        in_specs=[pl.BlockSpec(memory_space=pl.ANY)] * 3,
        out_specs=pl.BlockSpec(memory_space=pltpu.VMEM),
        scratch_shapes=[
            plane_stack(planes, lines, cells),
            plane_stack(planes, lines, cells),
            plane_stack(planes, lines, cells),
            plane_stack(planes, rows, 128),
            plane_stack(planes, rows, 128),
            plane_stack(planes, rows, 128),
            plane_stack(planes, rows, 128),
            plane_stack(planes, rows, 128),
            plane_stack(10, rows, 128),
            plane_stack(10, rows, 128),
            plane_stack(12, rows, 128),
            plane_stack(planes, rows, 128),
            plane_stack(planes, rows, 128),
            plane_stack(12, lines, WIDE),
            pltpu.VMEM((6, 10, lines, WIDE), jnp.float32),
            plane_stack(10, lines, WIDE),
            pltpu.VMEM((2, 10, lines, WIDE), jnp.float32),
            pltpu.VMEM((2, 8, lines, WIDE), jnp.float32),
            pltpu.VMEM((2, 6, lines, WIDE), jnp.float32),
            plane_stack(planes, lines, WIDE),
            pltpu.SemaphoreType.DMA((3,)),
            pltpu.SemaphoreType.DMA((20,)),
            pltpu.SemaphoreType.DMA((20,)),
        ],
        compiler_params=pltpu.CompilerParams(collective_id=0, has_side_effects=True, vmem_limit_bytes=(53 << 20) + (3 << 17)),
        cost_estimate=pl.CostEstimate(flops=20_000_000, bytes_accessed=1_200_000, transcendentals=0),
    )(targets, sources, permittivity)


def solution(mesh):
    in_specs = (P("blk", "bulk", None, None), P("blk", "bulk", None, None), P("bulk", None, None))
    out_specs = P("blk", "bulk", None, None)
    return jax.shard_map(
        functools.partial(shards, mesh.shape["blk"], mesh.shape["bulk"]),
        mesh=mesh, in_specs=in_specs, out_specs=out_specs, check_vma=False,
    )
```

```python
import functools
import math

import jax
import jax.numpy as jnp
from jax import lax
from jax.experimental import pallas as pl
from jax.experimental.pallas import tpu as pltpu
from jax.sharding import PartitionSpec as P

MESH = pl.DeviceIdType.MESH
SLAB = 4
WIDE = 256
SCALE = math.pi


def packed(plane):
    lines = plane.shape[0]
    right = plane[:, 128:192]
    return plane[:, 0:128], jnp.concatenate([right[: lines // 2], right[lines // 2 :]], axis=1)


def unpacked(both):
    lines = both.shape[0] * 2 // 3
    left, right = both[:lines], both[lines:]
    left_turned = pltpu.roll(left, 64, 1)
    right_turned = pltpu.roll(right, 64, 1)
    lane = lax.broadcasted_iota(jnp.int32, right.shape, 1)
    low = jnp.where(lane < 64, right, jnp.where(lane < 96, left_turned[: lines // 2], right_turned))
    high = jnp.where(lane < 64, right_turned, jnp.where(lane < 96, left_turned[lines // 2 :], right))
    return left, jnp.concatenate([low, high], axis=0)


def each(start, count, body):
    def step(i, carry):
        body(start + i)
        return carry
    lax.fori_loop(0, count, step, 0, unroll=True)


def ahead(cells, axis):
    return pltpu.roll(cells, cells.shape[axis] - 1, axis)


def behind(cells, axis):
    return pltpu.roll(cells, 1, axis)


def kernel(
    n_blk, n_bulk,
    t_hbm, s_hbm, e_hbm, out_ref,
    t_in, s_in, e_in, own_s, own_t, tgt, near_s, next_s, near_rhs, next_rhs, eps, done, back, eps_wide, coef, inverse, first, mid, late, total,
    in_sem, send_sem, recv_sem,
):
    b, k = lax.axis_index("blk"), lax.axis_index("bulk")
    pos, core, z, hi = b // 2, lax.rem(b, 2), k // 2, lax.rem(k, 2)
    n_pos, n_z = n_blk // 2, n_bulk // 2
    lines = t_in.shape[1]

    def worker(at, which, layer, side):
        return at * 2 + 1 - side, 2 * layer + 1 - which

    side, which = 1 - core, 1 - hi
    home = side == hi
    away = side != hi
    prev_pos, next_pos = lax.rem(pos + n_pos - 1, n_pos), lax.rem(pos + 1, n_pos)
    mate = (b + 1 - 2 * core, k)
    beyond = (b + 1 - 2 * core, lax.rem(z + n_z - 1 + 2 * side, n_z) * 2 + hi)
    swap = (b + 1 - 2 * core, k + 1 - 2 * hi)
    beside = (b + 2 - 4 * lax.rem(pos, 2), k + 1 - 2 * hi)
    n_x = n_blk // 4
    share = SLAB // n_x
    alike = [(lax.rem(b + 4 * j, n_blk), k) for j in range(n_x)]
    to_one = worker(lax.rem(pos + core, n_pos), 1 - core, z, hi)
    to_two = worker(next_pos, core, z, hi)
    from_one = (lax.rem(pos + n_pos - 1 + which, n_pos) * 2 + 1 - which, 2 * z + side)
    from_two = (prev_pos * 2 + which, 2 * z + side)

    loads = [
        pltpu.make_async_copy(src, dst, in_sem.at[i])
        for i, (src, dst) in enumerate(((s_hbm.at[0], s_in), (t_hbm.at[0], t_in), (e_hbm, e_in)))
    ]
    for load in loads:
        load.start()

    barrier = pltpu.get_barrier_semaphore()

    def tell(devices):
        for device in devices:
            pl.semaphore_signal(barrier, inc=1, device_id=device, device_id_type=MESH)

    tell((from_one, from_two, mate, beyond))

    @pl.when(away)
    def _():
        tell((swap, beside))

    def pack(src, dst, at):
        def body(i):
            left, right = packed(src[i])
            dst[at + i, 0:lines] = left
            dst[at + i, lines:] = right
        each(0, SLAB, body)

    def copy(i, src, src_at, dst, dst_at, count, device, rows=slice(None)):
        return pltpu.make_async_remote_copy(
            src_ref=src.at[pl.ds(src_at, count), rows], dst_ref=dst.at[pl.ds(dst_at, count), rows],
            send_sem=send_sem.at[i], recv_sem=recv_sem.at[i], device_id=device, device_id_type=MESH,
        )

    def relays(i, buf, rows=slice(None)):
        return (
            copy(i, buf, 4 - side, buf, 7 * side, 3, mate, rows),
            copy(i + 1, buf, 3 + side, buf, 7 * (1 - side), 3, beyond, rows),
        )

    half = own_s.shape[1] // 2
    parts = (slice(0, half), slice(half, 2 * half))

    source_one = copy(0, own_s, 0, near_s, 0, SLAB, to_one)
    source_two = [copy(i, own_s, 0, next_s, 0, SLAB, to_two, rows) for i, rows in zip((1, 14), parts)]
    target = copy(2, own_t, 0, tgt, 0, SLAB, swap)
    perm = copy(3, eps, 4, eps, 4, SLAB, beside)
    near_mate, near_beyond = relays(4, near_rhs)
    next_mate, next_beyond = zip(*(relays(i, next_rhs, rows) for i, rows in zip((6, 15), parts)))
    eps_mate = copy(8, eps, 4, eps, 8 * side, SLAB, mate)
    eps_beyond = copy(9, eps, 4, eps, 8 * (1 - side), SLAB, beyond)

    def result(i):
        return copy(10 + i, done, i, back, i, 1, swap)

    loads[0].wait()
    pack(s_in, own_s, 0)
    loads[1].wait()
    loads[2].wait()

    @pl.when(away)
    def _():
        pack(t_in, own_t, 0)

    @pl.when(home)
    def _():
        pack(t_in, tgt, 0)
        pack(e_in, eps, 4)

    pl.semaphore_wait(barrier, 5)

    def wide_body(i):
        left, right = unpacked(eps[i])
        eps_wide[i, :, 0:128] = left
        eps_wide[i, :, 128:WIDE] = right

    def coef_body(i):
        cells = eps_wide[i + 1]
        ahead_x = 0.5 * (cells + ahead(cells, 0))
        ahead_y = 0.5 * (cells + ahead(cells, 1))
        ahead_z = 0.5 * (cells + eps_wide[i + 2])
        behind_x = behind(ahead_x, 0)
        behind_y = behind(ahead_y, 1)
        behind_z = 0.5 * (cells + eps_wide[i])
        inv = 1.0 / (ahead_x + behind_x + ahead_y + behind_y + ahead_z + behind_z)
        inverse[i] = SCALE * inv
        for j, face in enumerate((ahead_x, behind_x, ahead_y, behind_y, ahead_z, behind_z)):
            coef[j, i] = face * inv

    def product(source, rhs, rows=slice(None)):
        def body(i):
            rhs[3 + i, rows] = source[i, rows] * tgt[i, rows]
        each(0, SLAB, body)

    @pl.when(home)
    def _():
        perm.start()
        source_one.start()
        eps_beyond.start()
        eps_mate.start()

    @pl.when(away)
    def _():
        source_one.start()
        target.start()
        perm.wait_recv()
        eps_beyond.start()
        eps_mate.start()
        target.wait_recv()

    source_one.wait_recv()
    product(near_s, near_rhs)
    near_beyond.start()
    near_mate.start()
    source_two[0].start()
    source_two[1].start()

    eps_mate.wait_recv()
    each(4 * (1 - side), 8, wide_body)
    each(4 * (1 - side), 6, coef_body)

    for i, rows in enumerate(parts):
        source_two[i].wait_recv()
        product(next_s, next_rhs, rows)
        next_beyond[i].start()
        next_mate[i].start()

    def swept(j, src, i, start):
        cells = src[j, i]
        near = first[j, start] + coef[0, start] * ahead(cells, 0) + coef[1, start] * behind(cells, 0)
        near = near + coef[2, start] * ahead(cells, 1) + coef[3, start] * behind(cells, 1)
        return near + coef[4, start] * src[j, i + 1] + coef[5, start] * src[j, i - 1]

    def first_body(j, rhs, i):
        left, right = unpacked(rhs[i])
        first[j, i, :, 0:128] = left * inverse[i, :, 0:128]
        first[j, i, :, 128:WIDE] = right * inverse[i, :, 128:WIDE]

    def mid_body(j, i):
        mid[j, i] = swept(j, first, i + 1, i + 1)

    def late_body(j, i):
        late[j, i] = swept(j, mid, i + 1, i + 2)

    def weighted(j, source, i):
        potential = swept(j, late, i + 1, i + 3)
        left, right = unpacked(source[i])
        return left * potential[:, 0:128], right * potential[:, 128:WIDE]

    def sooner(j, rhs, arrivals):
        for arrival in arrivals:
            arrival.wait_recv()
        each(4 * (1 - side), 6, functools.partial(first_body, j, rhs))
        each(4 * (1 - side), 4, functools.partial(mid_body, j))
        each(4 * (1 - side), 2, functools.partial(late_body, j))

    def later(j, rhs, arrivals):
        for arrival in arrivals:
            arrival.wait_recv()
        each(6 * side, 4, functools.partial(first_body, j, rhs))
        each(4 * side, 4, functools.partial(mid_body, j))
        each(2 * side, 4, functools.partial(late_body, j))

    def near_out(i):
        total[i, :, 0:128], total[i, :, 128:WIDE] = weighted(0, near_s, i)

    def hand_over(i):
        left, right = weighted(1, next_s, i)
        left = -(total[i, :, 0:128] + left)
        right = -(total[i, :, 128:WIDE] + right)

        @pl.when(home)
        def _():
            out_ref[0, i, :, 0:128] = left
            out_ref[0, i, :, 128:192] = right[:, 0:64]

        @pl.when(away)
        def _():
            done[i, 0:lines] = left
            done[i, lines:] = jnp.concatenate([right[: lines // 2, 0:64], right[lines // 2 :, 0:64]], axis=1)
            result(i).start()

    sooner(0, near_rhs, (near_mate,))
    sooner(1, next_rhs, next_mate)
    eps_beyond.wait_recv()
    each(8 * side, 4, wide_body)
    each(6 * side, 4, coef_body)
    later(0, near_rhs, (near_beyond,))
    each(0, SLAB, near_out)
    later(1, next_rhs, next_beyond)
    for i in range(SLAB):
        hand_over(i)

    for sent in (source_one, *source_two, near_mate, near_beyond, *next_mate, *next_beyond, eps_mate, eps_beyond):
        sent.wait_send()

    @pl.when(home)
    def _():
        perm.wait_send()

    @pl.when(away)
    def _():
        target.wait_send()

        def back_body(i):
            result(i).wait()
            left, right = unpacked(back[i])
            out_ref[0, i, :, 0:128] = left
            out_ref[0, i, :, 128:192] = right[:, 0:64]

        each(0, SLAB, back_body)


def shards(n_blk, n_bulk, targets, sources, permittivity):
    _, planes, lines, cells = targets.shape
    rows = lines * cells // 128

    def plane_stack(count, *tile):
        return pltpu.VMEM((count, *tile), jnp.float32)

    return pl.pallas_call(
        functools.partial(kernel, n_blk, n_bulk),
        out_shape=jax.ShapeDtypeStruct(targets.shape, jnp.float32),
        in_specs=[pl.BlockSpec(memory_space=pl.ANY)] * 3,
        out_specs=pl.BlockSpec(memory_space=pltpu.VMEM),
        scratch_shapes=[
            plane_stack(planes, lines, cells),
            plane_stack(planes, lines, cells),
            plane_stack(planes, lines, cells),
            plane_stack(planes, rows, 128),
            plane_stack(planes, rows, 128),
            plane_stack(planes, rows, 128),
            plane_stack(planes, rows, 128),
            plane_stack(planes, rows, 128),
            plane_stack(10, rows, 128),
            plane_stack(10, rows, 128),
            plane_stack(12, rows, 128),
            plane_stack(planes, rows, 128),
            plane_stack(planes, rows, 128),
            plane_stack(12, lines, WIDE),
            pltpu.VMEM((6, 10, lines, WIDE), jnp.float32),
            plane_stack(10, lines, WIDE),
            pltpu.VMEM((2, 10, lines, WIDE), jnp.float32),
            pltpu.VMEM((2, 8, lines, WIDE), jnp.float32),
            pltpu.VMEM((2, 6, lines, WIDE), jnp.float32),
            plane_stack(planes, lines, WIDE),
            pltpu.SemaphoreType.DMA((3,)),
            pltpu.SemaphoreType.DMA((20,)),
            pltpu.SemaphoreType.DMA((20,)),
        ],
        compiler_params=pltpu.CompilerParams(collective_id=0, has_side_effects=True, vmem_limit_bytes=(53 << 20) + (3 << 17)),
        cost_estimate=pl.CostEstimate(flops=20_000_000, bytes_accessed=1_200_000, transcendentals=0),
    )(targets, sources, permittivity)


def solution(mesh):
    in_specs = (P("blk", "bulk", None, None), P("blk", "bulk", None, None), P("bulk", None, None))
    out_specs = P("blk", "bulk", None, None)
    return jax.shard_map(
        functools.partial(shards, mesh.shape["blk"], mesh.shape["bulk"]),
        mesh=mesh, in_specs=in_specs, out_specs=out_specs, check_vma=False,
    )
```

```python
import functools
import math

import jax
import jax.numpy as jnp
from jax import lax
from jax.experimental import pallas as pl
from jax.experimental.pallas import tpu as pltpu
from jax.sharding import PartitionSpec as P

MESH = pl.DeviceIdType.MESH
SLAB = 4
WIDE = 256
SCALE = math.pi


def packed(plane):
    lines = plane.shape[0]
    right = plane[:, 128:192]
    return plane[:, 0:128], jnp.concatenate([right[: lines // 2], right[lines // 2 :]], axis=1)


def unpacked(both):
    lines = both.shape[0] * 2 // 3
    left, right = both[:lines], both[lines:]
    left_turned = pltpu.roll(left, 64, 1)
    right_turned = pltpu.roll(right, 64, 1)
    lane = lax.broadcasted_iota(jnp.int32, right.shape, 1)
    low = jnp.where(lane < 64, right, jnp.where(lane < 96, left_turned[: lines // 2], right_turned))
    high = jnp.where(lane < 64, right_turned, jnp.where(lane < 96, left_turned[lines // 2 :], right))
    return left, jnp.concatenate([low, high], axis=0)


def each(start, count, body):
    def step(i, carry):
        body(start + i)
        return carry
    lax.fori_loop(0, count, step, 0, unroll=True)


def ahead(cells, axis):
    return pltpu.roll(cells, cells.shape[axis] - 1, axis)


def behind(cells, axis):
    return pltpu.roll(cells, 1, axis)


def kernel(
    n_blk, n_bulk,
    t_hbm, s_hbm, e_hbm, out_ref,
    t_in, s_in, e_in, own_s, own_t, tgt, near_s, next_s, near_rhs, next_rhs, eps, done, back, eps_wide, coef, inverse, first, mid, late, total,
    in_sem, send_sem, recv_sem,
):
    b, k = lax.axis_index("blk"), lax.axis_index("bulk")
    pos, core, z, hi = b // 2, lax.rem(b, 2), k // 2, lax.rem(k, 2)
    n_pos, n_z = n_blk // 2, n_bulk // 2
    lines = t_in.shape[1]

    def worker(at, which, layer, side):
        return at * 2 + 1 - side, 2 * layer + 1 - which

    side, which = 1 - core, 1 - hi
    home = side == hi
    away = side != hi
    prev_pos, next_pos = lax.rem(pos + n_pos - 1, n_pos), lax.rem(pos + 1, n_pos)
    mate = (b + 1 - 2 * core, k)
    beyond = (b + 1 - 2 * core, lax.rem(z + n_z - 1 + 2 * side, n_z) * 2 + hi)
    swap = (b + 1 - 2 * core, k + 1 - 2 * hi)
    beside = (b + 2 - 4 * lax.rem(pos, 2), k + 1 - 2 * hi)
    n_x = n_blk // 4
    share = SLAB // n_x
    alike = [(lax.rem(b + 4 * j, n_blk), k) for j in range(n_x)]
    to_one = worker(lax.rem(pos + core, n_pos), 1 - core, z, hi)
    to_two = worker(next_pos, core, z, hi)
    from_one = (lax.rem(pos + n_pos - 1 + which, n_pos) * 2 + 1 - which, 2 * z + side)
    from_two = (prev_pos * 2 + which, 2 * z + side)

    loads = [
        pltpu.make_async_copy(src, dst, in_sem.at[i])
        for i, (src, dst) in enumerate(((s_hbm.at[0], s_in), (t_hbm.at[0], t_in), (e_hbm, e_in)))
    ]
    for load in loads:
        load.start()

    barrier = pltpu.get_barrier_semaphore()

    def tell(devices):
        for device in devices:
            pl.semaphore_signal(barrier, inc=1, device_id=device, device_id_type=MESH)

    tell((from_one, from_two, mate, beyond))

    @pl.when(away)
    def _():
        tell((swap, beside))

    def pack(src, dst, at):
        def body(i):
            left, right = packed(src[i])
            dst[at + i, 0:lines] = left
            dst[at + i, lines:] = right
        each(0, SLAB, body)

    def copy(i, src, src_at, dst, dst_at, count, device, rows=slice(None)):
        return pltpu.make_async_remote_copy(
            src_ref=src.at[pl.ds(src_at, count), rows], dst_ref=dst.at[pl.ds(dst_at, count), rows],
            send_sem=send_sem.at[i], recv_sem=recv_sem.at[i], device_id=device, device_id_type=MESH,
        )

    def relays(i, buf, rows=slice(None)):
        return (
            copy(i, buf, 4 - side, buf, 7 * side, 3, mate, rows),
            copy(i + 1, buf, 3 + side, buf, 7 * (1 - side), 3, beyond, rows),
        )

    half = own_s.shape[1] // 2
    parts = (slice(0, half), slice(half, 2 * half))

    source_one = [copy(i, own_s, 0, near_s, 0, SLAB, to_one, rows) for i, rows in zip((0, 17), parts)]
    source_two = [copy(i, own_s, 0, next_s, 0, SLAB, to_two, rows) for i, rows in zip((1, 14), parts)]
    target = copy(2, own_t, 0, tgt, 0, SLAB, swap)
    perm = copy(3, eps, 4, eps, 4, SLAB, beside)
    near_mate, near_beyond = zip(*(relays(i, near_rhs, rows) for i, rows in zip((4, 18), parts)))
    next_mate, next_beyond = zip(*(relays(i, next_rhs, rows) for i, rows in zip((6, 15), parts)))
    eps_mate = copy(8, eps, 4, eps, 8 * side, SLAB, mate)
    eps_beyond = copy(9, eps, 4, eps, 8 * (1 - side), SLAB, beyond)

    def result(i):
        return copy(10 + i, done, i, back, i, 1, swap)

    loads[0].wait()
    pack(s_in, own_s, 0)
    loads[1].wait()
    loads[2].wait()

    @pl.when(away)
    def _():
        pack(t_in, own_t, 0)

    @pl.when(home)
    def _():
        pack(t_in, tgt, 0)
        pack(e_in, eps, 4)

    pl.semaphore_wait(barrier, 5)

    def wide_body(i):
        left, right = unpacked(eps[i])
        eps_wide[i, :, 0:128] = left
        eps_wide[i, :, 128:WIDE] = right

    def coef_body(i):
        cells = eps_wide[i + 1]
        ahead_x = 0.5 * (cells + ahead(cells, 0))
        ahead_y = 0.5 * (cells + ahead(cells, 1))
        ahead_z = 0.5 * (cells + eps_wide[i + 2])
        behind_x = behind(ahead_x, 0)
        behind_y = behind(ahead_y, 1)
        behind_z = 0.5 * (cells + eps_wide[i])
        inv = 1.0 / (ahead_x + behind_x + ahead_y + behind_y + ahead_z + behind_z)
        inverse[i] = SCALE * inv
        for j, face in enumerate((ahead_x, behind_x, ahead_y, behind_y, ahead_z, behind_z)):
            coef[j, i] = face * inv

    def product(source, rhs, rows=slice(None)):
        def body(i):
            rhs[3 + i, rows] = source[i, rows] * tgt[i, rows]
        each(0, SLAB, body)

    @pl.when(home)
    def _():
        perm.start()
        source_one[0].start()
        source_one[1].start()
        eps_beyond.start()
        eps_mate.start()

    @pl.when(away)
    def _():
        source_one[0].start()
        source_one[1].start()
        target.start()
        perm.wait_recv()
        eps_beyond.start()
        eps_mate.start()
        target.wait_recv()

    for i, rows in enumerate(parts):
        source_one[i].wait_recv()
        product(near_s, near_rhs, rows)
        near_beyond[i].start()
        near_mate[i].start()
        source_two[i].start()

    eps_mate.wait_recv()
    each(4 * (1 - side), 8, wide_body)
    each(4 * (1 - side), 6, coef_body)

    for i, rows in enumerate(parts):
        source_two[i].wait_recv()
        product(next_s, next_rhs, rows)
        next_beyond[i].start()
        next_mate[i].start()

    def swept(j, src, i, start):
        cells = src[j, i]
        near = first[j, start] + coef[0, start] * ahead(cells, 0) + coef[1, start] * behind(cells, 0)
        near = near + coef[2, start] * ahead(cells, 1) + coef[3, start] * behind(cells, 1)
        return near + coef[4, start] * src[j, i + 1] + coef[5, start] * src[j, i - 1]

    def first_body(j, rhs, i):
        left, right = unpacked(rhs[i])
        first[j, i, :, 0:128] = left * inverse[i, :, 0:128]
        first[j, i, :, 128:WIDE] = right * inverse[i, :, 128:WIDE]

    def mid_body(j, i):
        mid[j, i] = swept(j, first, i + 1, i + 1)

    def late_body(j, i):
        late[j, i] = swept(j, mid, i + 1, i + 2)

    def weighted(j, source, i):
        potential = swept(j, late, i + 1, i + 3)
        left, right = unpacked(source[i])
        return left * potential[:, 0:128], right * potential[:, 128:WIDE]

    def sooner(j, rhs, arrivals):
        for arrival in arrivals:
            arrival.wait_recv()
        each(4 * (1 - side), 6, functools.partial(first_body, j, rhs))
        each(4 * (1 - side), 4, functools.partial(mid_body, j))
        each(4 * (1 - side), 2, functools.partial(late_body, j))

    def later(j, rhs, arrivals):
        for arrival in arrivals:
            arrival.wait_recv()
        each(6 * side, 4, functools.partial(first_body, j, rhs))
        each(4 * side, 4, functools.partial(mid_body, j))
        each(2 * side, 4, functools.partial(late_body, j))

    def near_out(i):
        total[i, :, 0:128], total[i, :, 128:WIDE] = weighted(0, near_s, i)

    def hand_over(i):
        left, right = weighted(1, next_s, i)
        left = -(total[i, :, 0:128] + left)
        right = -(total[i, :, 128:WIDE] + right)

        @pl.when(home)
        def _():
            out_ref[0, i, :, 0:128] = left
            out_ref[0, i, :, 128:192] = right[:, 0:64]

        @pl.when(away)
        def _():
            done[i, 0:lines] = left
            done[i, lines:] = jnp.concatenate([right[: lines // 2, 0:64], right[lines // 2 :, 0:64]], axis=1)
            result(i).start()

    sooner(0, near_rhs, near_mate)
    sooner(1, next_rhs, next_mate)
    eps_beyond.wait_recv()
    each(8 * side, 4, wide_body)
    each(6 * side, 4, coef_body)
    later(0, near_rhs, near_beyond)
    each(0, SLAB, near_out)
    later(1, next_rhs, next_beyond)
    for i in range(SLAB):
        hand_over(i)

    for sent in (*source_one, *source_two, *near_mate, *near_beyond, *next_mate, *next_beyond, eps_mate, eps_beyond):
        sent.wait_send()

    @pl.when(home)
    def _():
        perm.wait_send()

    @pl.when(away)
    def _():
        target.wait_send()

        def back_body(i):
            result(i).wait()
            left, right = unpacked(back[i])
            out_ref[0, i, :, 0:128] = left
            out_ref[0, i, :, 128:192] = right[:, 0:64]

        each(0, SLAB, back_body)


def shards(n_blk, n_bulk, targets, sources, permittivity):
    _, planes, lines, cells = targets.shape
    rows = lines * cells // 128

    def plane_stack(count, *tile):
        return pltpu.VMEM((count, *tile), jnp.float32)

    return pl.pallas_call(
        functools.partial(kernel, n_blk, n_bulk),
        out_shape=jax.ShapeDtypeStruct(targets.shape, jnp.float32),
        in_specs=[pl.BlockSpec(memory_space=pl.ANY)] * 3,
        out_specs=pl.BlockSpec(memory_space=pltpu.VMEM),
        scratch_shapes=[
            plane_stack(planes, lines, cells),
            plane_stack(planes, lines, cells),
            plane_stack(planes, lines, cells),
            plane_stack(planes, rows, 128),
            plane_stack(planes, rows, 128),
            plane_stack(planes, rows, 128),
            plane_stack(planes, rows, 128),
            plane_stack(planes, rows, 128),
            plane_stack(10, rows, 128),
            plane_stack(10, rows, 128),
            plane_stack(12, rows, 128),
            plane_stack(planes, rows, 128),
            plane_stack(planes, rows, 128),
            plane_stack(12, lines, WIDE),
            pltpu.VMEM((6, 10, lines, WIDE), jnp.float32),
            plane_stack(10, lines, WIDE),
            pltpu.VMEM((2, 10, lines, WIDE), jnp.float32),
            pltpu.VMEM((2, 8, lines, WIDE), jnp.float32),
            pltpu.VMEM((2, 6, lines, WIDE), jnp.float32),
            plane_stack(planes, lines, WIDE),
            pltpu.SemaphoreType.DMA((3,)),
            pltpu.SemaphoreType.DMA((20,)),
            pltpu.SemaphoreType.DMA((20,)),
        ],
        compiler_params=pltpu.CompilerParams(collective_id=0, has_side_effects=True, vmem_limit_bytes=(53 << 20) + (3 << 17)),
        cost_estimate=pl.CostEstimate(flops=20_000_000, bytes_accessed=1_200_000, transcendentals=0),
    )(targets, sources, permittivity)


def solution(mesh):
    in_specs = (P("blk", "bulk", None, None), P("blk", "bulk", None, None), P("bulk", None, None))
    out_specs = P("blk", "bulk", None, None)
    return jax.shard_map(
        functools.partial(shards, mesh.shape["blk"], mesh.shape["bulk"]),
        mesh=mesh, in_specs=in_specs, out_specs=out_specs, check_vma=False,
    )
```
